32 devices in a mesh: groups: 2 (over y), frame: 4 (over z), map: 2 (over x), psf: 2 (over core).
Axes of the slice: x: 2, y: 2, z: 4, core: 2. Of those that a mesh axis runs over, the one named last changes fastest.
Arguments:
- observed: float32 [8, 128, 512], P(('groups', 'frame'), ('map', 'psf')), parts along dimension 0, may hold values from -6 to 6
- pixel_mask: int32 [8, 128, 512], P(('groups', 'frame'), ('map', 'psf')), parts along dimension 0, may hold values 0 or 1
- ramp_counts: int32 [8, 128, 512], P(('groups', 'frame'), ('map', 'psf')), parts along dimension 0, may hold values from 1 to 16
- flat_map: float32 [8, 32, 512], P(('groups', 'map', 'psf'), 'frame'), parts along dimension 0, may hold values from 0.5 to 1.5
- bfe_map: float32 [8, 32, 512], P(('groups', 'map', 'psf'), 'frame'), parts along dimension 0, may hold values from 0.005 to 0.05
- ipc_kernel: float32 [6, 3], P('groups'), parts along dimension 0, may hold values from 0 to 0.04
- zernike: float32 [42], P('groups'), parts along dimension 0, may hold values from -2.5 to 2.5
- jitter: float32 [8], P(('groups', 'frame')), parts along dimension 0, may hold values from 4 to 20
- sky_level: float32 [8], P(('groups', 'frame')), parts along dimension 0, may hold values from 0.5 to 2
- dither: int32 [8, 2], P(('groups', 'frame')), parts along dimension 0, may hold values from -56 to 55
Outputs:
- grad_flat: float32 [8, 32, 512], P(('groups', 'map', 'psf'), 'frame'), parts along dimension 0
- grad_bfe: float32 [8, 32, 512], P(('groups', 'map', 'psf'), 'frame'), parts along dimension 0
- grad_ipc: float32 [6, 3], P('groups'), parts along dimension 0
- grad_zernike: float32 [42], P('groups'), parts along dimension 0
- grad_jitter: float32 [8], P(('groups', 'frame')), parts along dimension 0
The draws below stay inside these ranges and needn't reach their ends.
There are 2 independent parts, one for each index of `groups`. The reference program is written for one: setup_inputs(seed, part) draws one part's arguments, and reference() takes and returns one part's arrays. A program takes and returns all parts, laid end to end along the dimension named above; each array names one. Nothing has to cross between parts.
All inputs are finite; a program needn't handle non-finite values. No bound on the sum of `pixel_mask` on one device may be relied on, other than what follows from the above.
Results may differ from the reference program's by a relative error of at most 0.0003.
Values sent between devices are 32-bit elements; how exact they have to be, the bound alone decides.
A program may use at most 64 MiB of HBM per device.

```python
import math
import jax
import jax.numpy as jnp
import numpy as np
from jax import lax

W = 512
NP = 256
NZ = 21
NR = 16
RD = 32
NB = 4
R = 128
NF = 4


def place_ends(result, key, smallest, top_value):
    longest = result.shape.index(max(result.shape))
    spots = []
    for shift in (0, 1):
        where = [jax.random.randint(jax.random.fold_in(key, axis), (), 0, length) for axis, length in enumerate(result.shape)]
        where[longest] = (where[longest] + shift) % result.shape[longest]
        spots.append(tuple(where))
    return result.at[spots[0]].set(smallest).at[spots[1]].set(top_value)


def shard_levels(own_key, extent, pieces, low, largest):
    loudness, own = 1.0, jax.random.fold_in(own_key, 6)
    for position, blocks in pieces:
        steps = jnp.exp(jax.random.uniform(jax.random.fold_in(own, position), (blocks,), jnp.float32, low / len(pieces), largest / len(pieces)))
        loudness = loudness * jnp.repeat(steps, extent[position] // blocks).reshape([-1 if axis == position else 1 for axis in range(len(extent))])
    return loudness


def gaussian(key, dims, width, most, cuts=(), held_as=jnp.bfloat16):
    loudness = shard_levels(key, dims, cuts, -0.22, 0.18) if cuts else 1.0
    result = jax.random.normal(key, dims, jnp.float32) * width * loudness
    return jnp.minimum(jnp.maximum(result, -most), most).astype(held_as)


def setup_inputs(seed: int = 0, part: int = 0) -> dict:
    key_list = jax.random.split(jax.random.key(seed), 11)
    part_keys = jax.random.split(jax.random.fold_in(key_list[10], part), 11)
    observed = gaussian(part_keys[0], (NF, R, W), 1.0, 6.0, ((0, 4), (1, 4)), jnp.float32)
    pixel_mask = place_ends((jax.random.randint(part_keys[1], (NF, R, W), 0, 16) < 15).astype(jnp.int32), jax.random.fold_in(part_keys[1], 1), 0, 1)
    ramp_counts = place_ends(jax.random.randint(part_keys[2], (NF, R, W), 1, NR + 1), jax.random.fold_in(part_keys[2], 1), 1, NR).astype(jnp.int32)
    flat_map = jnp.clip(1.0 + 0.1 * jax.random.normal(part_keys[3], (NB, RD, W), jnp.float32), 0.5, 1.5)
    bfe_map = jnp.clip(jnp.exp(math.log(0.05) - 2.3025851 * jax.random.uniform(part_keys[4], (NB, RD, W), jnp.float32) ** shard_levels(part_keys[4], (NB, RD, W), ((0, 4), (1, 4)), -0.2, 0.2)), 0.005, 0.05)
    ipc_kernel = jnp.clip(jax.random.uniform(part_keys[5], (3, 3), jnp.float32, 0.0, 0.04), 0.0, 0.04)
    zernike = gaussian(part_keys[6], (NZ,), 0.4, 2.5, (), jnp.float32)
    jitter = jnp.clip(jnp.exp(math.log(20.0) - 1.609438 * jax.random.uniform(part_keys[7], (NF,), jnp.float32) ** shard_levels(part_keys[7], (NF,), ((0, 4),), -0.2, 0.2)), 4.0, 20.0)
    sky_level = jnp.clip(0.5 + 1.5 * jax.random.uniform(part_keys[8], (NF,), jnp.float32) ** shard_levels(part_keys[8], (NF,), ((0, 4),), -0.2, 0.2), 0.5, 2.0)
    dither = place_ends(jax.random.randint(part_keys[9], (NF, 2), 8 - min(R, W) // 2, min(R, W) // 2 - 8), jax.random.fold_in(part_keys[9], 1), 8 - min(R, W) // 2, (min(R, W) // 2 - 8) - 1).astype(jnp.int32)
    return {"observed": observed, "pixel_mask": pixel_mask, "ramp_counts": ramp_counts, "flat_map": flat_map, "bfe_map": bfe_map, "ipc_kernel": ipc_kernel, "zernike": zernike, "jitter": jitter, "sky_level": sky_level, "dither": dither}


HIGHEST_PRECISION = lax.Precision.HIGHEST
OVERSAMPLE = 32.0
AMPLITUDE = 2.0
IPC_CENTER = 0.8

def bfe_table():
    table_values = np.zeros((5, 5))
    for i in range(5):
        for j in range(5):
            distance = (i - 2) ** 2 + (j - 2) ** 2
            if distance > 0:
                table_values[i, j] = 1.0 / distance
    table_values[2, 2] = -table_values.sum()
    return table_values / -table_values[2, 2]

def center_table():
    table_values = np.zeros((3, 3))
    table_values[1, 1] = IPC_CENTER
    return table_values

def correlate(padded, kernel):
    kernel_size = kernel.shape[0]
    half_size = kernel_size // 2
    out_rows = padded.shape[-2] - 2 * half_size
    columns = padded.shape[-1]
    extended = jnp.pad(padded, [(0, 0)] * (padded.ndim - 1) + [(half_size, half_size)])
    accum_sum = jnp.zeros(padded.shape[:-2] + (out_rows, columns), padded.dtype)
    for i in range(kernel_size):
        for j in range(kernel_size):
            accum_sum = accum_sum + kernel[i, j] * extended[..., i:i + out_rows, j:j + columns]
    return accum_sum

def pupil_modes(coords):
    mode_list = []
    for degree in range(6):
        for power in range(degree + 1):
            mode_list.append(jnp.outer(coords ** power, coords ** (degree - power)))
    return jnp.stack(mode_list, 0)

def frame_image(zernike, jitter_width, sky_value, shift_row, shift_col, row_pos, total_rows, npupil, columns):
    coords = (2.0 * jnp.arange(npupil, dtype=jnp.float32) + 1.0) / npupil - 1.0
    pupil_phase = jnp.tensordot(zernike, pupil_modes(coords), axes=1, precision=HIGHEST_PRECISION)
    radius = coords[:, None] ** 2 + coords[None, :] ** 2
    aperture = jnp.where((radius <= 1.0) & (radius >= 0.09), 1.0, 0.0).astype(jnp.float32)
    pupil_real = aperture * jnp.cos(pupil_phase)
    pupil_imag = aperture * jnp.sin(pupil_phase)
    rho = total_rows / 2.0 + shift_row.astype(jnp.float32)
    chi = columns / 2.0 + shift_col.astype(jnp.float32)
    col_pos = jnp.arange(columns, dtype=jnp.float32)
    left_angle = -math.pi * (row_pos - rho)[:, None] * coords[None, :] / OVERSAMPLE
    right_angle = -math.pi * coords[:, None] * (col_pos - chi)[None, :] / OVERSAMPLE
    left_real, left_imag = (jnp.cos(left_angle), jnp.sin(left_angle))
    right_real, right_imag = (jnp.cos(right_angle), jnp.sin(right_angle))
    mid_real = jnp.dot(left_real, pupil_real, precision=HIGHEST_PRECISION) - jnp.dot(left_imag, pupil_imag, precision=HIGHEST_PRECISION)
    mid_imag = jnp.dot(left_real, pupil_imag, precision=HIGHEST_PRECISION) + jnp.dot(left_imag, pupil_real, precision=HIGHEST_PRECISION)
    field_real = jnp.dot(mid_real, right_real, precision=HIGHEST_PRECISION) - jnp.dot(mid_imag, right_imag, precision=HIGHEST_PRECISION)
    field_imag = jnp.dot(mid_real, right_imag, precision=HIGHEST_PRECISION) + jnp.dot(mid_imag, right_real, precision=HIGHEST_PRECISION)
    intensity = (field_real * field_real + field_imag * field_imag) * (AMPLITUDE / npupil ** 2) ** 2
    offsets = col_pos[:, None] - col_pos[None, :]
    blur = jnp.exp(-offsets * offsets / (2.0 * jitter_width * jitter_width))
    blur = blur / lax.optimization_barrier(jnp.sum(blur, axis=0, keepdims=True))
    return jnp.dot(intensity, blur, precision=HIGHEST_PRECISION) + sky_value

def reference(observed, pixel_mask, ramp_counts, flat_map, bfe_map, ipc_kernel, zernike, jitter, sky_level, dither):
    frames, total_rows, columns = observed.shape
    flat_gain = flat_map.reshape(total_rows, columns)
    bfe_gain = bfe_map.reshape(total_rows, columns)
    weights = pixel_mask.astype(jnp.float32) * ramp_counts.astype(jnp.float32) / NR / math.sqrt(frames)
    row_pos = jnp.arange(total_rows, dtype=jnp.float32)
    bfe_kernel = jnp.asarray(bfe_table(), jnp.float32)
    center_kernel = jnp.asarray(center_table(), jnp.float32)

    def frame_loss(flat_gain, bfe_gain, ipc_kernel, zernike, jitter_width, sky_value, shift, observed_frame, frame_weights):
        psf_image = frame_image(zernike, jitter_width, sky_value, shift[0], shift[1], row_pos, total_rows, NP, columns)
        charge = flat_gain * psf_image
        curvature = correlate(jnp.pad(charge, ((2, 2), (0, 0))), bfe_kernel)
        spread = charge * (1.0 + bfe_gain * curvature)
        detected = correlate(jnp.pad(spread, ((1, 1), (0, 0))), ipc_kernel + center_kernel)
        residual = detected - observed_frame
        return 0.5 * jnp.sum(frame_weights * residual * residual)
    gradient_fn = jax.grad(frame_loss, argnums=(0, 1, 2, 3, 4))

    def frame_step(running, inputs):
        jitter_width, sky_value, shift, observed_frame, frame_weights = inputs
        grad_flat, grad_bfe, grad_ipc, grad_zern, grad_width = gradient_fn(flat_gain, bfe_gain, ipc_kernel, zernike, jitter_width, sky_value, shift, observed_frame, frame_weights)
        return ((running[0] + grad_flat, running[1] + grad_bfe, running[2] + grad_ipc, running[3] + grad_zern), grad_width)
    start_sums = (jnp.zeros((total_rows, columns), jnp.float32), jnp.zeros((total_rows, columns), jnp.float32), jnp.zeros((3, 3), jnp.float32), jnp.zeros(zernike.shape, jnp.float32))
    sums_out, grad_widths = lax.scan(frame_step, start_sums, (jitter, sky_level, dither, observed, weights))
    return (sums_out[0].reshape(flat_map.shape), sums_out[1].reshape(bfe_map.shape), sums_out[2], sums_out[3], grad_widths)
```

```python
import functools
import math

import jax
import jax.numpy as jnp
import numpy as np
from jax import lax
from jax.experimental import pallas as pl
from jax.experimental.pallas import tpu as pltpu
from jax.sharding import PartitionSpec as P

NP = 256
NR = 16
HALO = 8
OVERSAMPLE = 32
AMPLITUDE = 2.0
IPC_CENTER = 0.8
DEGREE = 5
F32 = jnp.float32
BF16 = jnp.bfloat16
MESH = pl.DeviceIdType.MESH


def turn_polynomials():
    nodes = 0.125 * (1.0 + np.cos((np.arange(64) + 0.5) * np.pi / 64))
    root = np.sqrt(nodes)
    cos_fit = np.polynomial.Chebyshev.fit(nodes, np.cos(2 * np.pi * root), 7, domain=[0, 0.25])
    sin_fit = np.polynomial.Chebyshev.fit(nodes, np.sin(2 * np.pi * root) / root, 7, domain=[0, 0.25])
    as_power = np.polynomial.Polynomial
    return (
        [float(v) for v in cos_fit.convert(kind=as_power).coef],
        [float(v) for v in sin_fit.convert(kind=as_power).coef],
    )


COS_COEF, SIN_COEF = turn_polynomials()


def horner(coefs, x):
    acc = jnp.full_like(x, coefs[-1])
    for value in coefs[-2::-1]:
        acc = acc * x + value
    return acc


def cos_sin_turns(turns):
    rest = turns - jnp.floor(turns + 0.5)
    square = rest * rest
    return horner(COS_COEF, square), rest * horner(SIN_COEF, square)


def bfe_weights():
    table = np.zeros((3, 3))
    total = 0.0
    for i in range(-2, 3):
        for j in range(-2, 3):
            if i or j:
                table[abs(i), abs(j)] = 1.0 / (i * i + j * j)
                total += 1.0 / (i * i + j * j)
    table[0, 0] = -total
    return (table / total).tolist()


BFE = bfe_weights()


def split(x):
    high = x.astype(BF16)
    return high, (x - high.astype(F32)).astype(BF16)


def mm(a, b, dims=((1,), (0,))):
    return lax.dot_general(a, b, (dims, ((), ())), preferred_element_type=F32)


def dot3(a, b_high, b_low, dims=((1,), (0,))):
    high, low = split(a)
    n = a.shape[0]
    both = mm(jnp.concatenate([high, low], 0), b_high, dims)
    return both[:n] + both[n:] + mm(high, b_low, dims)


def iota(shape, axis):
    return lax.broadcasted_iota(jnp.int32, shape, axis).astype(F32)


def repeat(count, body):
    if count <= 16:
        for i in range(count):
            body(i)
    else:
        lax.fori_loop(0, count, lambda i, c: (body(i), c)[1], 0)


def kernel(
    nf, nmap, npsf, rd, k, width,
    zern, jit, sky, dith, ipc, flat_in, bfe_in, obs_in, mask_in, count_in,
    gflat, gbfe, small,
    maps, ow, obs_v, mask_v, count_v, pup, ph, plo, bh, bl, gh, gl, dh, dl, gout, gin, outbox, inbox,
    local_sem, map_send, map_recv, ow_send, ow_recv, rs_send, rs_recv, box_send, box_recv,
):
    nb = nmap * npsf
    group = nf * nb
    rows = rd + 2 * HALO
    h = HALO // k
    f = lax.axis_index("frame")
    m = lax.axis_index("map")
    p = lax.axis_index("psf")
    b = m * npsf + p
    me = f * nb + b

    def device(frame, block):
        return {"frame": frame, "map": block // npsf, "psf": block % npsf}

    def peer(offset):
        other = lax.rem(me + offset, group)
        return other, device(other // nb, other % nb)

    barrier = pltpu.get_barrier_semaphore()

    def greet(i):
        pl.semaphore_signal(barrier, inc=1, device_id=peer(i + 1)[1], device_id_type=MESH)

    repeat(group - 1, greet)

    loads = [
        pltpu.make_async_copy(flat_in.at[0], maps.at[h + f, 0], local_sem.at[0]),
        pltpu.make_async_copy(bfe_in.at[0], maps.at[h + f, 1], local_sem.at[1]),
        pltpu.make_async_copy(obs_in.at[0], obs_v, local_sem.at[2]),
        pltpu.make_async_copy(mask_in.at[0], mask_v, local_sem.at[3]),
        pltpu.make_async_copy(count_in.at[0], count_v, local_sem.at[4]),
    ]
    for load in loads:
        load.start()

    step = 64
    lane_u = (2.0 * iota((1, NP), 1) + 1.0) / NP - 1.0
    lane_pow = [jnp.ones((1, NP), F32)]
    for _ in range(DEGREE):
        lane_pow.append(lane_pow[-1] * lane_u)
    per_power = []
    for power in range(DEGREE + 1):
        acc = jnp.zeros((1, NP), F32)
        for q in range(DEGREE + 1 - power):
            d = power + q
            acc = acc + (zern[d * (d + 1) // 2 + power] * (0.5 / math.pi)) * lane_pow[q]
        per_power.append(acc)

    def pupil(i, carry):
        start = pl.multiple_of(i * step, step)
        u = (2.0 * (iota((step, NP), 0) + (i * step).astype(F32)) + 1.0) / NP - 1.0
        turns = jnp.broadcast_to(per_power[DEGREE], (step, NP))
        for power in range(DEGREE - 1, -1, -1):
            turns = turns * u + per_power[power]
        radius = u * u + lane_u * lane_u
        inside = jnp.where((radius <= 1.0) & (radius >= 0.09), 1.0, 0.0)
        real, imag = cos_sin_turns(turns)
        for half, value in enumerate((real * inside, imag * inside)):
            at = (pl.ds(start, step), pl.ds(half * NP, NP))
            high, low = split(value)
            pup[at] = value
            ph[at] = high
            plo[at] = low
        return carry

    lax.fori_loop(0, NP // step, pupil, 0)

    for load in loads:
        load.wait()
    scale = 1.0 / (NR * math.sqrt(nf))
    blocks = rd // 8
    ow[1 : 1 + blocks, 0] = obs_v[...].reshape(blocks, 8, width)
    weight = mask_v[...].astype(F32) * count_v[...].astype(F32) * scale
    ow[1 : 1 + blocks, 1] = weight.reshape(blocks, 8, width)

    @pl.when(b == 0)
    def _():
        maps[0:h] = jnp.zeros((h, 2, k, width), F32)
        ow[0:1] = jnp.zeros((1, 2, 8, width), F32)

    @pl.when(b == nb - 1)
    def _():
        maps[h + nf : 2 * h + nf] = jnp.zeros((h, 2, k, width), F32)
        ow[1 + blocks : 2 + blocks] = jnp.zeros((1, 2, 8, width), F32)

    pl.semaphore_wait(barrier, group - 1)

    def remote(src, dst, send, recv, where):
        return pltpu.make_async_remote_copy(
            src_ref=src, dst_ref=dst, send_sem=send, recv_sem=recv, device_id=where, device_id_type=MESH
        )

    has_up = b > 0
    has_down = b < nb - 1
    gives_down = has_down & (f >= nf - h)
    gives_up = has_up & (f < h)
    mine = maps.at[h + f]

    def ow_up():
        return remote(ow.at[1], ow.at[1 + blocks], ow_send.at[0], ow_recv.at[1], device(f, b - 1))

    def ow_down():
        return remote(ow.at[blocks], ow.at[0], ow_send.at[1], ow_recv.at[0], device(f, b + 1))

    def map_same(i):
        return remote(
            mine, maps.at[h + f], map_send.at[0, i], map_recv.at[h + f], device(lax.rem(f + i + 1, nf), b)
        )

    def map_down(i):
        slot = f - (nf - h)
        return remote(
            mine, maps.at[slot], map_send.at[1, i], map_recv.at[slot], device(lax.rem(f + i, nf), b + 1)
        )

    def map_up(i):
        slot = h + nf + f
        return remote(
            mine, maps.at[slot], map_send.at[2, i], map_recv.at[slot], device(lax.rem(f + i, nf), b - 1)
        )

    repeat(nf - 1, lambda i: map_same(i).start())

    @pl.when(gives_down)
    def _():
        repeat(nf, lambda i: map_down(i).start())

    @pl.when(gives_up)
    def _():
        repeat(nf, lambda i: map_up(i).start())

    @pl.when(has_up)
    def _():
        ow_up().start()

    @pl.when(has_down)
    def _():
        ow_down().start()

    rho = nb * rd / 2.0 + dith[0, 0].astype(F32)
    chi = width / 2.0 + dith[0, 1].astype(F32)
    unit = 1.0 / (2 * OVERSAMPLE * NP)
    col_step = 32

    def column(i, carry):
        start = pl.multiple_of(i * col_step, col_step)
        index = 2.0 * (iota((col_step, width), 0) + (i * col_step).astype(F32)) + (1.0 - NP)
        turns = index * (chi - iota((col_step, width), 1)) * unit
        for half, value in enumerate(cos_sin_turns(turns)):
            at = (pl.ds(start, col_step), pl.ds(half * width, width))
            high, low = split(value)
            bh[at] = high
            bl[at] = low
        return carry

    lax.fori_loop(0, NP // col_step, column, 0)

    sigma = jnp.full((1, width), jit[0], F32)
    inv = 1.0 / sigma
    inv2 = inv * inv
    cube = inv2 * inv

    def blur(i, carry):
        total, total_dot = carry
        start = pl.multiple_of(i * col_step, col_step)
        off = iota((col_step, width), 0) + (i * col_step).astype(F32) - iota((col_step, width), 1)
        square = off * off
        value = jnp.exp(square * (-0.5 * inv2))
        slope = value * (square * cube)
        at = (pl.ds(start, col_step), slice(None))
        gh[at], gl[at] = split(value)
        dh[at], dl[at] = split(slope)
        total = total + jnp.sum(value.reshape(col_step // 8, 8, width), 0)
        total_dot = total_dot + jnp.sum(slope.reshape(col_step // 8, 8, width), 0)
        return total, total_dot

    zero8 = jnp.zeros((8, width), F32)
    total, total_dot = lax.fori_loop(0, width // col_step, blur, (zero8, zero8))
    inv_total = 1.0 / jnp.sum(total, 0, keepdims=True)
    ratio = jnp.sum(total_dot, 0, keepdims=True) * inv_total

    first = (b * rd).astype(F32) - float(HALO)
    row_angle = (2.0 * iota((rows, NP), 1) + (1.0 - NP)) * (rho - first - iota((rows, NP), 0)) * unit
    a_real, a_imag = cos_sin_turns(row_angle)
    left = jnp.concatenate([a_real, a_imag], 0)
    x = dot3(left, ph[...], plo[...])
    mid = jnp.concatenate(
        [x[:rows, :NP] - x[rows:, NP:], x[:rows, NP:] + x[rows:, :NP]], 0
    )
    y = dot3(mid, bh[...], bl[...])
    e_real = y[:rows, :width] - y[rows:, width:]
    e_imag = y[:rows, width:] + y[rows:, :width]
    norm = (AMPLITUDE / NP**2) ** 2
    intensity = (e_real * e_real + e_imag * e_imag) * norm
    own = slice(HALO, HALO + rd)
    blurred = dot3(intensity, gh[...], gl[...]) * inv_total
    blurred_dot = dot3(intensity[own], dh[...], dl[...]) * inv_total - blurred[own] * ratio
    image = blurred + sky[0]

    def arrive(i):
        @pl.when(i != f)
        def _():
            remote(mine, maps.at[h + i], map_send.at[0, 0], map_recv.at[h + i], device(f, b)).wait_recv()

    repeat(nf, arrive)

    @pl.when(has_up)
    def _():
        repeat(h, lambda i: remote(mine, maps.at[i], map_send.at[0, 0], map_recv.at[i], device(f, b)).wait_recv())
        ow_down().wait_recv()

    @pl.when(has_down)
    def _():
        repeat(
            h,
            lambda i: remote(
                mine, maps.at[h + nf + i], map_send.at[0, 0], map_recv.at[h + nf + i], device(f, b)
            ).wait_recv(),
        )
        ow_up().wait_recv()

    flat = maps[:, 0].reshape(rows, width)
    bfe = maps[:, 1].reshape(rows, width)
    observed = ow[:, 0].reshape(rows, width)
    weights = ow[:, 1].reshape(rows, width)
    col = lax.broadcasted_iota(jnp.int32, (rows, width), 1)

    def down(value, d):
        return pltpu.roll(value, (-d) % value.shape[0], 0)

    def across(value, d):
        rolled = pltpu.roll(value, (-d) % width, 1)
        at = col[: value.shape[0]]
        return jnp.where(at < width - d if d > 0 else at >= -d, rolled, 0.0)

    def curve(value):
        one = down(value, 1) + down(value, -1)
        two = down(value, 2) + down(value, -2)
        parts = [BFE[0][j] * value + BFE[1][j] * one + BFE[2][j] * two for j in range(3)]
        return (
            parts[0]
            + (across(parts[1], 1) + across(parts[1], -1))
            + (across(parts[2], 2) + across(parts[2], -2))
        )

    kappa = [[ipc[i, j] + (IPC_CENTER if i == j == 1 else 0.0) for j in range(3)] for i in range(3)]

    def couple(value, table):
        shifted = [down(value, -1), value, down(value, 1)]
        parts = [sum(table[i][j] * shifted[i] for i in range(3)) for j in range(3)]
        return parts[1] + across(parts[0], -1) + across(parts[2], 1)

    charge = flat * image
    curvature = curve(charge)
    gain = 1.0 + bfe * curvature
    spread = charge * gain
    resid = weights * (couple(spread, kappa) - observed)
    spread_grad = couple(resid, [row[::-1] for row in kappa[::-1]])
    scaled = spread_grad * charge
    charge_grad = (spread_grad * gain + curve(scaled * bfe))[own]
    gout[:, 1] = (scaled * curvature)[own].reshape(nf, k, width)
    gout[:, 0] = (charge_grad * image[own]).reshape(nf, k, width)

    def scatter(i):
        other = lax.rem(f + i + 1, nf)
        return remote(gout.at[other], gin.at[f], rs_send.at[i], rs_recv.at[f], device(other, b))

    repeat(nf - 1, lambda i: scatter(i).start())
    gin[f] = gout[f]

    image_grad = charge_grad * flat[own]
    dint = dot3(image_grad * inv_total, gh[...], gl[...]) * (2.0 * norm)
    de = jnp.concatenate([e_real[own] * dint, e_imag[own] * dint], 0)
    nt = ((1,), (1,))
    z_real = dot3(de, bh[:, :width], bl[:, :width], nt)
    z_imag = dot3(de, bh[:, width:], bl[:, width:], nt)
    dm_real = z_real[:rd] + z_imag[rd:]
    dm_imag = z_real[rd:] - z_imag[:rd]
    right = jnp.concatenate(
        [jnp.concatenate([dm_real, dm_imag], 1), jnp.concatenate([dm_imag, -dm_real], 1)], 0
    )
    right_high, right_low = split(right)
    left_own = jnp.concatenate([a_real[own], a_imag[own]], 0).T
    left_high, left_low = split(left_own)
    dp = (
        mm(left_high, right_high) + mm(left_low, right_high) + mm(left_high, right_low)
    )
    dphase = pup[:, :NP] * dp[:, NP:] - pup[:, NP:] * dp[:, :NP]
    full_u = (2.0 * iota((NP, NP), 0) + 1.0) / NP - 1.0
    term = dphase
    by_power = []
    for power in range(DEGREE + 1):
        by_power.append(jnp.sum(term, 0, keepdims=True))
        if power < DEGREE:
            term = term * full_u
    by_power.append(jnp.zeros((2, NP), F32))
    by_row = jnp.concatenate(by_power, 0)
    sub = lax.broadcasted_iota(jnp.int32, (8, 128), 0)
    lane = lax.broadcasted_iota(jnp.int32, (8, 128), 1)
    modes = jnp.zeros((8, 128), F32)
    for q in range(DEGREE + 1):
        value = jnp.sum(by_row * lane_pow[q], 1, keepdims=True)
        for power in range(DEGREE + 1 - q):
            d = power + q
            here = (sub == power) & (lane == d * (d + 1) // 2 + power)
            modes = jnp.where(here, value, modes)
    modes = jnp.sum(modes, 0, keepdims=True)

    def fold(value):
        folded = jnp.sum(value.reshape(rd // 8, 8, width), 0)
        return sum(folded[:, j * 128 : (j + 1) * 128] for j in range(width // 128))

    def everything(folded):
        return jnp.sum(jnp.sum(folded, 0, keepdims=True), 1, keepdims=True)

    tile = jnp.where(sub == 1, modes, 0.0)
    resid_own = resid[own]
    shifted_resid = [across(resid_own, 1), resid_own, across(resid_own, -1)]
    for i in range(3):
        spread_rows = spread[HALO + i - 1 : HALO + rd + i - 1]
        for j in range(3):
            value = everything(fold(shifted_resid[j] * spread_rows))
            tile = jnp.where((sub == 0) & (lane == 3 * i + j), value, tile)
    tile = jnp.where((sub == 2) & (lane == 0), everything(fold(image_grad * blurred_dot)), tile)
    outbox[...] = tile

    def post(i):
        return remote(outbox, inbox.at[me], box_send.at[i], box_recv.at[me], peer(i + 1)[1])

    repeat(group - 1, lambda i: post(i).start())
    inbox[me] = tile

    def gathered(i):
        other = lax.rem(f + i + 1, nf)
        remote(gout.at[0], gin.at[other], rs_send.at[i], rs_recv.at[other], device(other, b)).wait_recv()

    repeat(nf - 1, gathered)
    summed = jnp.sum(gin[...], 0)
    gflat[0] = summed[0]
    gbfe[0] = summed[1]

    def posted(i):
        other, where = peer(i + 1)
        remote(outbox, inbox.at[other], box_send.at[i], box_recv.at[other], where).wait_recv()

    repeat(group - 1, posted)
    of_frame = jnp.sum(inbox[pl.ds(f * nb, nb)], 0)
    small[...] = jnp.where(sub == 2, of_frame, jnp.sum(inbox[...], 0))

    repeat(nf - 1, lambda i: map_same(i).wait_send())

    @pl.when(gives_down)
    def _():
        repeat(nf, lambda i: map_down(i).wait_send())

    @pl.when(gives_up)
    def _():
        repeat(nf, lambda i: map_up(i).wait_send())

    @pl.when(has_up)
    def _():
        ow_up().wait_send()

    @pl.when(has_down)
    def _():
        ow_down().wait_send()

    repeat(nf - 1, lambda i: scatter(i).wait_send())
    repeat(group - 1, lambda i: post(i).wait_send())


def local(
    nf, nmap, npsf,
    observed, pixel_mask, ramp_counts, flat_map, bfe_map, ipc_kernel, zernike, jitter, sky_level, dither,
):
    _, rd, width = observed.shape
    k = flat_map.shape[1]
    group = nf * nmap * npsf
    h = HALO // k
    smem = pl.BlockSpec(memory_space=pltpu.SMEM)
    hbm = pl.BlockSpec(memory_space=pl.ANY)
    vmem = pl.BlockSpec(memory_space=pltpu.VMEM)
    dma = pltpu.SemaphoreType.DMA
    gflat, gbfe, small = pl.pallas_call(
        functools.partial(kernel, nf, nmap, npsf, rd, k, width),
        out_shape=(
            jax.ShapeDtypeStruct((1, k, width), F32),
            jax.ShapeDtypeStruct((1, k, width), F32),
            jax.ShapeDtypeStruct((8, 128), F32),
        ),
        in_specs=[smem] * 5 + [hbm] * 5,
        out_specs=(vmem, vmem, vmem),
        scratch_shapes=[
            pltpu.VMEM((nf + 2 * h, 2, k, width), F32),
            pltpu.VMEM((rd // 8 + 2, 2, 8, width), F32),
            pltpu.VMEM((rd, width), F32),
            pltpu.VMEM((rd, width), jnp.int32),
            pltpu.VMEM((rd, width), jnp.int32),
            pltpu.VMEM((NP, 2 * NP), F32),
            pltpu.VMEM((NP, 2 * NP), BF16),
            pltpu.VMEM((NP, 2 * NP), BF16),
            pltpu.VMEM((NP, 2 * width), BF16),
            pltpu.VMEM((NP, 2 * width), BF16),
            pltpu.VMEM((width, width), BF16),
            pltpu.VMEM((width, width), BF16),
            pltpu.VMEM((width, width), BF16),
            pltpu.VMEM((width, width), BF16),
            pltpu.VMEM((nf, 2, k, width), F32),
            pltpu.VMEM((nf, 2, k, width), F32),
            pltpu.VMEM((8, 128), F32),
            pltpu.VMEM((group, 8, 128), F32),
            dma((5,)),
            dma((3, nf)),
            dma((nf + 2 * h,)),
            dma((2,)),
            dma((2,)),
            dma((nf,)),
            dma((nf,)),
            dma((group,)),
            dma((group,)),
        ],
        compiler_params=pltpu.CompilerParams(
            collective_id=0, has_side_effects=True, vmem_limit_bytes=40 * 1024 * 1024
        ),
    )(zernike, jitter, sky_level, dither, ipc_kernel, flat_map, bfe_map, observed, pixel_mask, ramp_counts)
    return (gflat, gbfe, small[0, :9].reshape(3, 3), small[1, : zernike.shape[0]], small[2, :1])


def solution(mesh):
    in_specs = (
        P(("groups", "frame"), ("map", "psf"), None),
        P(("groups", "frame"), ("map", "psf"), None),
        P(("groups", "frame"), ("map", "psf"), None),
        P(("groups", "map", "psf"), "frame", None),
        P(("groups", "map", "psf"), "frame", None),
        P("groups", None),
        P("groups"),
        P(("groups", "frame")),
        P(("groups", "frame")),
        P(("groups", "frame"), None),
    )
    out_specs = (
        P(("groups", "map", "psf"), "frame", None),
        P(("groups", "map", "psf"), "frame", None),
        P("groups", None),
        P("groups"),
        P(("groups", "frame")),
    )
    body = functools.partial(local, mesh.shape["frame"], mesh.shape["map"], mesh.shape["psf"])
    return jax.shard_map(body, mesh=mesh, in_specs=in_specs, out_specs=out_specs, check_vma=False)
```

```python
import functools
import math

import jax
import jax.numpy as jnp
import numpy as np
from jax import lax
from jax.experimental import pallas as pl
from jax.experimental.pallas import tpu as pltpu
from jax.sharding import PartitionSpec as P

NP = 256
NR = 16
HALO = 8
VMEM_LIMIT = 63 * 1024 * 1024
OVERSAMPLE = 32
AMPLITUDE = 2.0
IPC_CENTER = 0.8
DEGREE = 5
F32 = jnp.float32
BF16 = jnp.bfloat16
MESH = pl.DeviceIdType.MESH


def turn_polynomials():
    nodes = 0.125 * (1.0 + np.cos((np.arange(64) + 0.5) * np.pi / 64))
    root = np.sqrt(nodes)
    cos_fit = np.polynomial.Chebyshev.fit(nodes, np.cos(2 * np.pi * root), 7, domain=[0, 0.25])
    sin_fit = np.polynomial.Chebyshev.fit(nodes, np.sin(2 * np.pi * root) / root, 7, domain=[0, 0.25])
    as_power = np.polynomial.Polynomial
    return (
        [float(v) for v in cos_fit.convert(kind=as_power).coef],
        [float(v) for v in sin_fit.convert(kind=as_power).coef],
    )


COS_COEF, SIN_COEF = turn_polynomials()


def horner(coefs, x):
    acc = jnp.full_like(x, coefs[-1])
    for value in coefs[-2::-1]:
        acc = acc * x + value
    return acc


def cos_sin_turns(turns):
    rest = turns - jnp.floor(turns + 0.5)
    square = rest * rest
    return horner(COS_COEF, square), rest * horner(SIN_COEF, square)


def bfe_weights():
    table = np.zeros((3, 3))
    total = 0.0
    for i in range(-2, 3):
        for j in range(-2, 3):
            if i or j:
                table[abs(i), abs(j)] = 1.0 / (i * i + j * j)
                total += 1.0 / (i * i + j * j)
    table[0, 0] = -total
    return (table / total).tolist()


BFE = bfe_weights()


def split(x):
    high = x.astype(BF16)
    return high, (x - high.astype(F32)).astype(BF16)


def mm(a, b, dims=((1,), (0,))):
    return lax.dot_general(a, b, (dims, ((), ())), preferred_element_type=F32)


def dot3(a, b_high, b_low, dims=((1,), (0,))):
    high, low = split(a)
    n = a.shape[0]
    both = mm(jnp.concatenate([high, low], 0), b_high, dims)
    return both[:n] + both[n:] + mm(high, b_low, dims)


def iota(shape, axis):
    return lax.broadcasted_iota(jnp.int32, shape, axis).astype(F32)


def repeat(count, body):
    if count <= 16:
        for i in range(count):
            body(i)
    else:
        lax.fori_loop(0, count, lambda i, c: (body(i), c)[1], 0)


def kernel(
    nf, nmap, npsf, rd, k, width,
    zern_in, jit_in, sky_in, dith_in, ipc_in, flat_in, bfe_in, obs_in, mask_in, count_in,
    gsum, small,
    zern, jit, sky, dith, ipc,
    maps, ow, obs_v, mask_v, count_v, pup, ph, plo, bh, bl, gh, gl, dh, dl, gout, gin, outbox, inbox,
    local_sem, map_send, pass_send, map_recv, ow_send, ow_recv, rs_send, rs_recv, box_send, box_recv,
):
    nb = nmap * npsf
    group = nf * nb
    rows = rd + 2 * HALO
    h = HALO // k
    f = lax.axis_index("frame")
    m = lax.axis_index("map")
    p = lax.axis_index("psf")
    b = m * npsf + p
    me = f * nb + b

    def device(frame, block):
        return {"frame": frame, "map": block // npsf, "psf": block % npsf}

    def peer(offset):
        other = lax.rem(me + offset, group)
        return other, device(other // nb, other % nb)

    barrier = pltpu.get_barrier_semaphore()

    def greet(i):
        pl.semaphore_signal(barrier, inc=1, device_id=peer(i + 1)[1], device_id_type=MESH)

    repeat(group - 1, greet)

    loads = [
        pltpu.make_async_copy(flat_in.at[0], maps.at[h + f, 0], local_sem.at[0]),
        pltpu.make_async_copy(bfe_in.at[0], maps.at[h + f, 1], local_sem.at[1]),
        pltpu.make_async_copy(obs_in.at[0], obs_v, local_sem.at[2]),
        pltpu.make_async_copy(mask_in.at[0], mask_v, local_sem.at[3]),
        pltpu.make_async_copy(count_in.at[0], count_v, local_sem.at[4]),
        pltpu.make_async_copy(zern_in, zern, local_sem.at[5]),
        pltpu.make_async_copy(jit_in, jit, local_sem.at[6]),
        pltpu.make_async_copy(sky_in, sky, local_sem.at[7]),
        pltpu.make_async_copy(dith_in, dith, local_sem.at[8]),
        pltpu.make_async_copy(ipc_in, ipc, local_sem.at[9]),
    ]
    for load in loads:
        load.start()

    def remote(src, dst, send, recv, where):
        return pltpu.make_async_remote_copy(
            src_ref=src, dst_ref=dst, send_sem=send, recv_sem=recv, device_id=where, device_id_type=MESH
        )

    has_up = b > 0
    has_down = b < nb - 1
    blocks = rd // 8
    mine = maps.at[h + f]

    def ow_up():
        return remote(ow.at[1], ow.at[1 + blocks], ow_send.at[0], ow_recv.at[1], device(f, b - 1))

    def ow_down():
        return remote(ow.at[blocks], ow.at[0], ow_send.at[1], ow_recv.at[0], device(f, b + 1))

    def map_same(i):
        return remote(mine, maps.at[h + f], map_send.at[i], map_recv.at[h + f], device(lax.rem(f + i + 1, nf), b))

    def map_down(i):
        return remote(maps.at[nf + i], maps.at[i], pass_send.at[1, i], map_recv.at[i], device(f, b + 1))

    def map_up(i):
        slot = h + nf + i
        return remote(maps.at[h + i], maps.at[slot], pass_send.at[0, i], map_recv.at[slot], device(f, b - 1))

    def arrive(i):
        @pl.when(i != f)
        def _():
            remote(mine, maps.at[h + i], map_send.at[0], map_recv.at[h + i], device(f, b)).wait_recv()

    @pl.when(b == 0)
    def _():
        maps[0:h] = jnp.zeros((h, 2, k, width), F32)
        ow[0:1] = jnp.zeros((1, 2, 8, width), F32)

    @pl.when(b == nb - 1)
    def _():
        maps[h + nf : 2 * h + nf] = jnp.zeros((h, 2, k, width), F32)
        ow[1 + blocks : 2 + blocks] = jnp.zeros((1, 2, 8, width), F32)

    for load in loads[:2]:
        load.wait()
    pl.semaphore_wait(barrier, group - 1)
    repeat(nf - 1, lambda i: map_same(i).start())

    for load in loads[2:]:
        load.wait()
    scale = 1.0 / (NR * math.sqrt(nf))
    ow[1 : 1 + blocks, 0] = obs_v[...].reshape(blocks, 8, width)
    weight = mask_v[...].astype(F32) * count_v[...].astype(F32) * scale
    ow[1 : 1 + blocks, 1] = weight.reshape(blocks, 8, width)

    @pl.when(has_up)
    def _():
        ow_up().start()

    @pl.when(has_down)
    def _():
        ow_down().start()

    step = 64
    lane_u = (2.0 * iota((1, NP), 1) + 1.0) / NP - 1.0
    lane_pow = [jnp.ones((1, NP), F32)]
    for _ in range(DEGREE):
        lane_pow.append(lane_pow[-1] * lane_u)
    per_power = []
    for power in range(DEGREE + 1):
        acc = jnp.zeros((1, NP), F32)
        for q in range(DEGREE + 1 - power):
            d = power + q
            acc = acc + (zern[d * (d + 1) // 2 + power] * (0.5 / math.pi)) * lane_pow[q]
        per_power.append(acc)

    def pupil(i, carry):
        start = pl.multiple_of(i * step, step)
        u = (2.0 * (iota((step, NP), 0) + (i * step).astype(F32)) + 1.0) / NP - 1.0
        turns = jnp.broadcast_to(per_power[DEGREE], (step, NP))
        for power in range(DEGREE - 1, -1, -1):
            turns = turns * u + per_power[power]
        radius = u * u + lane_u * lane_u
        inside = jnp.where((radius <= 1.0) & (radius >= 0.09), 1.0, 0.0)
        real, imag = cos_sin_turns(turns)
        for half, value in enumerate((real * inside, imag * inside)):
            at = (pl.ds(start, step), pl.ds(half * NP, NP))
            high, low = split(value)
            pup[at] = value
            ph[at] = high
            plo[at] = low
        return carry

    lax.fori_loop(0, NP // step, pupil, 0)

    rho = nb * rd / 2.0 + dith[0, 0].astype(F32)
    chi = width / 2.0 + dith[0, 1].astype(F32)
    unit = 1.0 / (2 * OVERSAMPLE * NP)
    col_step = 32

    def column(i, carry):
        start = pl.multiple_of(i * col_step, col_step)
        index = 2.0 * (iota((col_step, width), 0) + (i * col_step).astype(F32)) + (1.0 - NP)
        turns = index * (chi - iota((col_step, width), 1)) * unit
        for half, value in enumerate(cos_sin_turns(turns)):
            at = (pl.ds(start, col_step), pl.ds(half * width, width))
            high, low = split(value)
            bh[at] = high
            bl[at] = low
        return carry

    lax.fori_loop(0, NP // col_step, column, 0)

    sigma = jnp.full((1, width), jit[0], F32)
    inv = 1.0 / sigma
    inv2 = inv * inv
    cube = inv2 * inv

    def blur(i, carry):
        total, total_dot = carry
        start = pl.multiple_of(i * col_step, col_step)
        off = iota((col_step, width), 0) + (i * col_step).astype(F32) - iota((col_step, width), 1)
        square = off * off
        value = jnp.exp(square * (-0.5 * inv2))
        slope = value * (square * cube)
        at = (pl.ds(start, col_step), slice(None))
        gh[at], gl[at] = split(value)
        dh[at], dl[at] = split(slope)
        total = total + jnp.sum(value.reshape(col_step // 8, 8, width), 0)
        total_dot = total_dot + jnp.sum(slope.reshape(col_step // 8, 8, width), 0)
        return total, total_dot

    zero8 = jnp.zeros((8, width), F32)
    total, total_dot = lax.fori_loop(0, width // col_step, blur, (zero8, zero8))
    inv_total = 1.0 / jnp.sum(total, 0, keepdims=True)
    ratio = jnp.sum(total_dot, 0, keepdims=True) * inv_total

    first = (b * rd).astype(F32) - float(HALO)
    row_angle = (2.0 * iota((rows, NP), 1) + (1.0 - NP)) * (rho - first - iota((rows, NP), 0)) * unit
    a_real, a_imag = cos_sin_turns(row_angle)
    left = jnp.concatenate([a_real, a_imag], 0)
    x = dot3(left, ph[...], plo[...])
    mid = jnp.concatenate(
        [x[:rows, :NP] - x[rows:, NP:], x[:rows, NP:] + x[rows:, :NP]], 0
    )
    y = dot3(mid, bh[...], bl[...])
    e_real = y[:rows, :width] - y[rows:, width:]
    e_imag = y[:rows, width:] + y[rows:, :width]
    norm = (AMPLITUDE / NP**2) ** 2
    intensity = (e_real * e_real + e_imag * e_imag) * norm
    own = slice(HALO, HALO + rd)

    repeat(h, arrive)
    repeat(h, lambda i: arrive(nf - h + i))

    @pl.when(has_up)
    def _():
        repeat(h, lambda i: map_up(i).start())

    @pl.when(has_down)
    def _():
        repeat(h, lambda i: map_down(i).start())

    blurred = dot3(intensity, gh[...], gl[...]) * inv_total
    blurred_dot = dot3(intensity[own], dh[...], dl[...]) * inv_total - blurred[own] * ratio
    image = blurred + sky[0]

    repeat(nf - 2 * h, lambda i: arrive(h + i))

    @pl.when(has_up)
    def _():
        repeat(h, lambda i: remote(mine, maps.at[i], map_send.at[0], map_recv.at[i], device(f, b)).wait_recv())
        ow_down().wait_recv()

    @pl.when(has_down)
    def _():
        repeat(
            h,
            lambda i: remote(
                mine, maps.at[h + nf + i], map_send.at[0], map_recv.at[h + nf + i], device(f, b)
            ).wait_recv(),
        )
        ow_up().wait_recv()

    flat = maps[:, 0].reshape(rows, width)
    bfe = maps[:, 1].reshape(rows, width)
    observed = ow[:, 0].reshape(rows, width)
    weights = ow[:, 1].reshape(rows, width)
    col = lax.broadcasted_iota(jnp.int32, (rows, width), 1)

    def down(value, d):
        return pltpu.roll(value, (-d) % value.shape[0], 0)

    def across(value, d):
        rolled = pltpu.roll(value, (-d) % width, 1)
        at = col[: value.shape[0]]
        return jnp.where(at < width - d if d > 0 else at >= -d, rolled, 0.0)

    def curve(value):
        one = down(value, 1) + down(value, -1)
        two = down(value, 2) + down(value, -2)
        parts = [BFE[0][j] * value + BFE[1][j] * one + BFE[2][j] * two for j in range(3)]
        return (
            parts[0]
            + (across(parts[1], 1) + across(parts[1], -1))
            + (across(parts[2], 2) + across(parts[2], -2))
        )

    kappa = [[ipc[i, j] + (IPC_CENTER if i == j == 1 else 0.0) for j in range(3)] for i in range(3)]

    def couple(value, table):
        shifted = [down(value, -1), value, down(value, 1)]
        parts = [sum(table[i][j] * shifted[i] for i in range(3)) for j in range(3)]
        return parts[1] + across(parts[0], -1) + across(parts[2], 1)

    charge = flat * image
    curvature = curve(charge)
    gain = 1.0 + bfe * curvature
    spread = charge * gain
    resid = weights * (couple(spread, kappa) - observed)
    spread_grad = couple(resid, [row[::-1] for row in kappa[::-1]])
    scaled = spread_grad * charge
    charge_grad = (spread_grad * gain + curve(scaled * bfe))[own]
    gout[:, 1] = (scaled * curvature)[own].reshape(nf, k, width)
    gout[:, 0] = (charge_grad * image[own]).reshape(nf, k, width)

    def scatter(i):
        other = lax.rem(f + i + 1, nf)
        return remote(gout.at[other], gin.at[f], rs_send.at[i], rs_recv.at[f], device(other, b))

    repeat(nf - 1, lambda i: scatter(i).start())
    gin[f] = gout[f]

    image_grad = charge_grad * flat[own]
    dint = dot3(image_grad * inv_total, gh[...], gl[...]) * (2.0 * norm)
    de = jnp.concatenate([e_real[own] * dint, e_imag[own] * dint], 0)
    nt = ((1,), (1,))
    z_real = dot3(de, bh[:, :width], bl[:, :width], nt)
    z_imag = dot3(de, bh[:, width:], bl[:, width:], nt)
    dm_real = z_real[:rd] + z_imag[rd:]
    dm_imag = z_real[rd:] - z_imag[:rd]
    right = jnp.concatenate(
        [jnp.concatenate([dm_real, dm_imag], 1), jnp.concatenate([dm_imag, -dm_real], 1)], 0
    )
    right_high, right_low = split(right)
    left_own = jnp.concatenate([a_real[own], a_imag[own]], 0).T
    left_high, left_low = split(left_own)
    dp = (
        mm(left_high, right_high) + mm(left_low, right_high) + mm(left_high, right_low)
    )
    dphase = pup[:, :NP] * dp[:, NP:] - pup[:, NP:] * dp[:, :NP]
    full_u = (2.0 * iota((NP, NP), 0) + 1.0) / NP - 1.0
    term = dphase
    by_power = []
    for power in range(DEGREE + 1):
        by_power.append(jnp.sum(term, 0, keepdims=True))
        if power < DEGREE:
            term = term * full_u
    by_power.append(jnp.zeros((2, NP), F32))
    by_row = jnp.concatenate(by_power, 0)
    sub = lax.broadcasted_iota(jnp.int32, (8, 128), 0)
    lane = lax.broadcasted_iota(jnp.int32, (8, 128), 1)
    modes = jnp.zeros((8, 128), F32)
    for q in range(DEGREE + 1):
        value = jnp.sum(by_row * lane_pow[q], 1, keepdims=True)
        for power in range(DEGREE + 1 - q):
            d = power + q
            here = (sub == power) & (lane == d * (d + 1) // 2 + power)
            modes = jnp.where(here, value, modes)
    modes = jnp.sum(modes, 0, keepdims=True)

    def fold(value):
        folded = jnp.sum(value.reshape(rd // 8, 8, width), 0)
        return sum(folded[:, j * 128 : (j + 1) * 128] for j in range(width // 128))

    def everything(folded):
        return jnp.sum(jnp.sum(folded, 0, keepdims=True), 1, keepdims=True)

    tile = jnp.where(sub == 3, modes, 0.0)
    resid_own = resid[own]
    shifted_resid = [across(resid_own, 1), resid_own, across(resid_own, -1)]
    for i in range(3):
        spread_rows = spread[HALO + i - 1 : HALO + rd + i - 1]
        for j in range(3):
            value = everything(fold(shifted_resid[j] * spread_rows))
            tile = jnp.where((sub == i) & (lane == j), value, tile)
    tile = jnp.where((sub == 4) & (lane == 0), everything(fold(image_grad * blurred_dot)), tile)
    outbox[...] = tile

    def post(i):
        return remote(outbox, inbox.at[me], box_send.at[i], box_recv.at[me], peer(i + 1)[1])

    repeat(group - 1, lambda i: post(i).start())
    inbox[me] = tile

    def gathered(i):
        other = lax.rem(f + i + 1, nf)
        remote(gout.at[0], gin.at[other], rs_send.at[i], rs_recv.at[other], device(other, b)).wait_recv()

    repeat(nf - 1, gathered)
    summed = jnp.sum(gin[...], 0)
    gsum[...] = summed

    def posted(i):
        other, where = peer(i + 1)
        remote(outbox, inbox.at[other], box_send.at[i], box_recv.at[other], where).wait_recv()

    repeat(group - 1, posted)
    of_frame = jnp.sum(inbox[pl.ds(f * nb, nb)], 0)
    small[...] = jnp.where(sub == 4, of_frame, jnp.sum(inbox[...], 0))

    repeat(nf - 1, lambda i: map_same(i).wait_send())

    @pl.when(has_up)
    def _():
        repeat(h, lambda i: map_up(i).wait_send())
        ow_up().wait_send()

    @pl.when(has_down)
    def _():
        repeat(h, lambda i: map_down(i).wait_send())
        ow_down().wait_send()

    repeat(nf - 1, lambda i: scatter(i).wait_send())
    repeat(group - 1, lambda i: post(i).wait_send())


def finish(gsum, small, gflat, gbfe, gipc, gzern, gjit):
    gflat[0] = gsum[0]
    gbfe[0] = gsum[1]
    gipc[...] = small[0:3, 0:3]
    gzern[...] = small[3, : gzern.shape[0]]
    gjit[...] = small[4, 0:1]


def local(
    nf, nmap, npsf,
    observed, pixel_mask, ramp_counts, flat_map, bfe_map, ipc_kernel, zernike, jitter, sky_level, dither,
):
    _, rd, width = observed.shape
    k = flat_map.shape[1]
    group = nf * nmap * npsf
    h = HALO // k
    hbm = pl.BlockSpec(memory_space=pl.ANY)
    vmem = pl.BlockSpec(memory_space=pltpu.VMEM)
    dma = pltpu.SemaphoreType.DMA
    gsum, small = pl.pallas_call(
        functools.partial(kernel, nf, nmap, npsf, rd, k, width),
        out_shape=(
            jax.ShapeDtypeStruct((2, k, width), F32),
            jax.ShapeDtypeStruct((8, 128), F32),
        ),
        in_specs=[hbm] * 10,
        out_specs=(vmem, vmem),
        scratch_shapes=[
            pltpu.SMEM(zernike.shape, F32),
            pltpu.SMEM((1,), F32),
            pltpu.SMEM((1,), F32),
            pltpu.SMEM((1, 2), jnp.int32),
            pltpu.SMEM((3, 3), F32),
            pltpu.VMEM((nf + 2 * h, 2, k, width), F32),
            pltpu.VMEM((rd // 8 + 2, 2, 8, width), F32),
            pltpu.VMEM((rd, width), F32),
            pltpu.VMEM((rd, width), jnp.int32),
            pltpu.VMEM((rd, width), jnp.int32),
            pltpu.VMEM((NP, 2 * NP), F32),
            pltpu.VMEM((NP, 2 * NP), BF16),
            pltpu.VMEM((NP, 2 * NP), BF16),
            pltpu.VMEM((NP, 2 * width), BF16),
            pltpu.VMEM((NP, 2 * width), BF16),
            pltpu.VMEM((width, width), BF16),
            pltpu.VMEM((width, width), BF16),
            pltpu.VMEM((width, width), BF16),
            pltpu.VMEM((width, width), BF16),
            pltpu.VMEM((nf, 2, k, width), F32),
            pltpu.VMEM((nf, 2, k, width), F32),
            pltpu.VMEM((8, 128), F32),
            pltpu.VMEM((group, 8, 128), F32),
            dma((10,)),
            dma((nf,)),
            dma((2, h)),
            dma((nf + 2 * h,)),
            dma((2,)),
            dma((2,)),
            dma((nf,)),
            dma((nf,)),
            dma((group,)),
            dma((group,)),
        ],
        compiler_params=pltpu.CompilerParams(
            collective_id=0, has_side_effects=True, vmem_limit_bytes=VMEM_LIMIT
        ),
    )(zernike, jitter, sky_level, dither, ipc_kernel, flat_map, bfe_map, observed, pixel_mask, ramp_counts)
    return pl.pallas_call(
        finish,
        out_shape=(
            jax.ShapeDtypeStruct(flat_map.shape, F32),
            jax.ShapeDtypeStruct(bfe_map.shape, F32),
            jax.ShapeDtypeStruct(ipc_kernel.shape, F32),
            jax.ShapeDtypeStruct(zernike.shape, F32),
            jax.ShapeDtypeStruct(jitter.shape, F32),
        ),
        in_specs=[vmem] * 2,
        out_specs=(vmem,) * 5,
    )(gsum, small)


def solution(mesh):
    in_specs = (
        P(("groups", "frame"), ("map", "psf"), None),
        P(("groups", "frame"), ("map", "psf"), None),
        P(("groups", "frame"), ("map", "psf"), None),
        P(("groups", "map", "psf"), "frame", None),
        P(("groups", "map", "psf"), "frame", None),
        P("groups", None),
        P("groups"),
        P(("groups", "frame")),
        P(("groups", "frame")),
        P(("groups", "frame"), None),
    )
    out_specs = (
        P(("groups", "map", "psf"), "frame", None),
        P(("groups", "map", "psf"), "frame", None),
        P("groups", None),
        P("groups"),
        P(("groups", "frame")),
    )
    body = functools.partial(local, mesh.shape["frame"], mesh.shape["map"], mesh.shape["psf"])
    return jax.shard_map(body, mesh=mesh, in_specs=in_specs, out_specs=out_specs, check_vma=False)
```

```python
import functools
import math

import jax
import jax.numpy as jnp
import numpy as np
from jax import lax
from jax.experimental import pallas as pl
from jax.experimental.pallas import tpu as pltpu
from jax.sharding import PartitionSpec as P

NP = 256
NR = 16
HALO = 8
VMEM_LIMIT = 63 * 1024 * 1024
OVERSAMPLE = 32
AMPLITUDE = 2.0
IPC_CENTER = 0.8
DEGREE = 5
F32 = jnp.float32
BF16 = jnp.bfloat16
MESH = pl.DeviceIdType.MESH


def turn_polynomials():
    nodes = 0.125 * (1.0 + np.cos((np.arange(64) + 0.5) * np.pi / 64))
    root = np.sqrt(nodes)
    cos_fit = np.polynomial.Chebyshev.fit(nodes, np.cos(2 * np.pi * root), 7, domain=[0, 0.25])
    sin_fit = np.polynomial.Chebyshev.fit(nodes, np.sin(2 * np.pi * root) / root, 7, domain=[0, 0.25])
    as_power = np.polynomial.Polynomial
    return (
        [float(v) for v in cos_fit.convert(kind=as_power).coef],
        [float(v) for v in sin_fit.convert(kind=as_power).coef],
    )


COS_COEF, SIN_COEF = turn_polynomials()


def horner(coefs, x):
    acc = jnp.full_like(x, coefs[-1])
    for value in coefs[-2::-1]:
        acc = acc * x + value
    return acc


def cos_sin_turns(turns):
    rest = turns - jnp.floor(turns + 0.5)
    square = rest * rest
    return horner(COS_COEF, square), rest * horner(SIN_COEF, square)


def bfe_weights():
    table = np.zeros((3, 3))
    total = 0.0
    for i in range(-2, 3):
        for j in range(-2, 3):
            if i or j:
                table[abs(i), abs(j)] = 1.0 / (i * i + j * j)
                total += 1.0 / (i * i + j * j)
    table[0, 0] = -total
    return (table / total).tolist()


BFE = bfe_weights()


def split(x):
    high = x.astype(BF16)
    return high, (x - high.astype(F32)).astype(BF16)


def mm(a, b, dims=((1,), (0,))):
    return lax.dot_general(a, b, (dims, ((), ())), preferred_element_type=F32)


def dot3(a, b_high, b_low, dims=((1,), (0,))):
    high, low = split(a)
    n = a.shape[0]
    both = mm(jnp.concatenate([high, low], 0), b_high, dims)
    return both[:n] + both[n:] + mm(high, b_low, dims)


def iota(shape, axis):
    return lax.broadcasted_iota(jnp.int32, shape, axis).astype(F32)


def repeat(count, body):
    if count <= 16:
        for i in range(count):
            body(i)
    else:
        lax.fori_loop(0, count, lambda i, c: (body(i), c)[1], 0)


def kernel(
    nf, nmap, npsf, rd, k, width,
    zern_in, level_in, dith_in, ipc_in, flat_in, bfe_in, obs_in, mask_in, count_in,
    gsum, small,
    zern, level, dith, ipc,
    maps, ow, obs_v, mask_v, count_v, pup, ph, plo, bh, bl, gh, gl, dh, dl, gout, gin, outbox, inbox,
    local_sem, map_send, pass_send, map_recv, ow_send, ow_recv, rs_send, rs_recv, box_send, box_recv,
):
    nb = nmap * npsf
    group = nf * nb
    rows = rd + 2 * HALO
    h = HALO // k
    f = lax.axis_index("frame")
    m = lax.axis_index("map")
    p = lax.axis_index("psf")
    b = m * npsf + p
    me = f * nb + b

    def device(frame, block):
        return {"frame": frame, "map": lax.div(block, npsf), "psf": lax.rem(block, npsf)}

    def wrap(value, count):
        return jnp.where(value >= count, value - count, value)

    others = [(i, j) for i in range(nmap) for j in range(npsf)]

    def each_peer(body):
        def of_frame(step, spots):
            for i, j in spots:
                body({"frame": wrap(f + step, nf), "map": wrap(m + i, nmap), "psf": wrap(p + j, npsf)})

        repeat(nf - 1, lambda step: of_frame(step + 1, others))
        of_frame(0, others[1:])

    barrier = pltpu.get_barrier_semaphore()
    each_peer(lambda where: pl.semaphore_signal(barrier, inc=1, device_id=where, device_id_type=MESH))

    loads = [
        pltpu.make_async_copy(flat_in.at[0], maps.at[h + f, 0], local_sem.at[0]),
        pltpu.make_async_copy(bfe_in.at[0], maps.at[h + f, 1], local_sem.at[1]),
        pltpu.make_async_copy(obs_in.at[0], obs_v, local_sem.at[2]),
        pltpu.make_async_copy(mask_in.at[0], mask_v, local_sem.at[3]),
        pltpu.make_async_copy(count_in.at[0], count_v, local_sem.at[4]),
        pltpu.make_async_copy(zern_in, zern, local_sem.at[5]),
        pltpu.make_async_copy(level_in, level, local_sem.at[6]),
        pltpu.make_async_copy(dith_in, dith, local_sem.at[7]),
        pltpu.make_async_copy(ipc_in, ipc, local_sem.at[8]),
    ]
    for load in loads:
        load.start()

    def remote(src, dst, send, recv, where):
        return pltpu.make_async_remote_copy(
            src_ref=src, dst_ref=dst, send_sem=send, recv_sem=recv, device_id=where, device_id_type=MESH
        )

    has_up = b > 0
    has_down = b < nb - 1
    blocks = rd // 8
    mine = maps.at[h + f]

    def ow_up():
        return remote(ow.at[1], ow.at[1 + blocks], ow_send.at[0], ow_recv.at[1], device(f, b - 1))

    def ow_down():
        return remote(ow.at[blocks], ow.at[0], ow_send.at[1], ow_recv.at[0], device(f, b + 1))

    def map_same(i):
        return remote(mine, maps.at[h + f], map_send.at[i], map_recv.at[h + f], device(lax.rem(f + i + 1, nf), b))

    def map_down(i):
        return remote(maps.at[nf + i], maps.at[i], pass_send.at[1, i], map_recv.at[i], device(f, b + 1))

    def map_up(i):
        slot = h + nf + i
        return remote(maps.at[h + i], maps.at[slot], pass_send.at[0, i], map_recv.at[slot], device(f, b - 1))

    def arrive(i):
        @pl.when(i != f)
        def _():
            remote(mine, maps.at[h + i], map_send.at[0], map_recv.at[h + i], device(f, b)).wait_recv()

    @pl.when(b == 0)
    def _():
        maps[0:h] = jnp.zeros((h, 2, k, width), F32)
        ow[0:1] = jnp.zeros((1, 2, 8, width), F32)

    @pl.when(b == nb - 1)
    def _():
        maps[h + nf : 2 * h + nf] = jnp.zeros((h, 2, k, width), F32)
        ow[1 + blocks : 2 + blocks] = jnp.zeros((1, 2, 8, width), F32)

    for load in loads[:2]:
        load.wait()
    pl.semaphore_wait(barrier, group - 1)
    repeat(nf - 1, lambda i: map_same(i).start())

    for load in loads[2:]:
        load.wait()
    scale = 1.0 / (NR * math.sqrt(nf))
    ow[1 : 1 + blocks, 0] = obs_v[...].reshape(blocks, 8, width)
    weight = mask_v[...].astype(F32) * count_v[...].astype(F32) * scale
    ow[1 : 1 + blocks, 1] = weight.reshape(blocks, 8, width)

    @pl.when(has_up)
    def _():
        ow_up().start()

    @pl.when(has_down)
    def _():
        ow_down().start()

    step = 64
    lane_u = (2.0 * iota((1, NP), 1) + 1.0) / NP - 1.0
    lane_pow = [jnp.ones((1, NP), F32)]
    for _ in range(DEGREE):
        lane_pow.append(lane_pow[-1] * lane_u)
    per_power = []
    for power in range(DEGREE + 1):
        acc = jnp.zeros((1, NP), F32)
        for q in range(DEGREE + 1 - power):
            d = power + q
            acc = acc + (zern[d * (d + 1) // 2 + power] * (0.5 / math.pi)) * lane_pow[q]
        per_power.append(acc)

    def pupil(i, carry):
        start = pl.multiple_of(i * step, step)
        u = (2.0 * (iota((step, NP), 0) + (i * step).astype(F32)) + 1.0) / NP - 1.0
        turns = jnp.broadcast_to(per_power[DEGREE], (step, NP))
        for power in range(DEGREE - 1, -1, -1):
            turns = turns * u + per_power[power]
        radius = u * u + lane_u * lane_u
        inside = jnp.where((radius <= 1.0) & (radius >= 0.09), 1.0, 0.0)
        real, imag = cos_sin_turns(turns)
        for half, value in enumerate((real * inside, imag * inside)):
            at = (pl.ds(start, step), pl.ds(half * NP, NP))
            high, low = split(value)
            pup[at] = value
            ph[at] = high
            plo[at] = low
        return carry

    lax.fori_loop(0, NP // step, pupil, 0)

    rho = nb * rd / 2.0 + dith[0, 0].astype(F32)
    chi = width / 2.0 + dith[0, 1].astype(F32)
    unit = 1.0 / (2 * OVERSAMPLE * NP)
    col_step = 32

    def column(i, carry):
        start = pl.multiple_of(i * col_step, col_step)
        index = 2.0 * (iota((col_step, width), 0) + (i * col_step).astype(F32)) + (1.0 - NP)
        turns = index * (chi - iota((col_step, width), 1)) * unit
        for half, value in enumerate(cos_sin_turns(turns)):
            at = (pl.ds(start, col_step), pl.ds(half * width, width))
            high, low = split(value)
            bh[at] = high
            bl[at] = low
        return carry

    lax.fori_loop(0, NP // col_step, column, 0)

    sigma = jnp.full((1, width), level[0], F32)
    inv = 1.0 / sigma
    inv2 = inv * inv
    cube = inv2 * inv

    def blur(i, carry):
        total, total_dot = carry
        start = pl.multiple_of(i * col_step, col_step)
        off = iota((col_step, width), 0) + (i * col_step).astype(F32) - iota((col_step, width), 1)
        square = off * off
        value = jnp.exp(square * (-0.5 * inv2))
        slope = value * (square * cube)
        at = (pl.ds(start, col_step), slice(None))
        gh[at], gl[at] = split(value)
        dh[at], dl[at] = split(slope)
        total = total + jnp.sum(value.reshape(col_step // 8, 8, width), 0)
        total_dot = total_dot + jnp.sum(slope.reshape(col_step // 8, 8, width), 0)
        return total, total_dot

    zero8 = jnp.zeros((8, width), F32)
    total, total_dot = lax.fori_loop(0, width // col_step, blur, (zero8, zero8))
    inv_total = 1.0 / jnp.sum(total, 0, keepdims=True)
    ratio = jnp.sum(total_dot, 0, keepdims=True) * inv_total

    first = (b * rd).astype(F32) - float(HALO)
    row_angle = (2.0 * iota((rows, NP), 1) + (1.0 - NP)) * (rho - first - iota((rows, NP), 0)) * unit
    a_real, a_imag = cos_sin_turns(row_angle)
    left = jnp.concatenate([a_real, a_imag], 0)
    x = dot3(left, ph[...], plo[...])
    mid = jnp.concatenate(
        [x[:rows, :NP] - x[rows:, NP:], x[:rows, NP:] + x[rows:, :NP]], 0
    )
    y = dot3(mid, bh[...], bl[...])
    e_real = y[:rows, :width] - y[rows:, width:]
    e_imag = y[:rows, width:] + y[rows:, :width]
    norm = (AMPLITUDE / NP**2) ** 2
    intensity = (e_real * e_real + e_imag * e_imag) * norm
    own = slice(HALO, HALO + rd)

    repeat(h, arrive)
    repeat(h, lambda i: arrive(nf - h + i))

    @pl.when(has_up)
    def _():
        repeat(h, lambda i: map_up(i).start())

    @pl.when(has_down)
    def _():
        repeat(h, lambda i: map_down(i).start())

    blurred = dot3(intensity, gh[...], gl[...]) * inv_total
    blurred_dot = dot3(intensity[own], dh[...], dl[...]) * inv_total - blurred[own] * ratio
    image = blurred + level[1]

    repeat(nf - 2 * h, lambda i: arrive(h + i))

    @pl.when(has_up)
    def _():
        repeat(h, lambda i: remote(mine, maps.at[i], map_send.at[0], map_recv.at[i], device(f, b)).wait_recv())
        ow_down().wait_recv()

    @pl.when(has_down)
    def _():
        repeat(
            h,
            lambda i: remote(
                mine, maps.at[h + nf + i], map_send.at[0], map_recv.at[h + nf + i], device(f, b)
            ).wait_recv(),
        )
        ow_up().wait_recv()

    flat = maps[:, 0].reshape(rows, width)
    bfe = maps[:, 1].reshape(rows, width)
    observed = ow[:, 0].reshape(rows, width)
    weights = ow[:, 1].reshape(rows, width)
    col = lax.broadcasted_iota(jnp.int32, (rows, width), 1)

    def down(value, d):
        return pltpu.roll(value, (-d) % value.shape[0], 0)

    def across(value, d):
        rolled = pltpu.roll(value, (-d) % width, 1)
        at = col[: value.shape[0]]
        return jnp.where(at < width - d if d > 0 else at >= -d, rolled, 0.0)

    def curve(value):
        one = down(value, 1) + down(value, -1)
        two = down(value, 2) + down(value, -2)
        parts = [BFE[0][j] * value + BFE[1][j] * one + BFE[2][j] * two for j in range(3)]
        return (
            parts[0]
            + (across(parts[1], 1) + across(parts[1], -1))
            + (across(parts[2], 2) + across(parts[2], -2))
        )

    kappa = [[ipc[i, j] + (IPC_CENTER if i == j == 1 else 0.0) for j in range(3)] for i in range(3)]

    def couple(value, table):
        shifted = [down(value, -1), value, down(value, 1)]
        parts = [sum(table[i][j] * shifted[i] for i in range(3)) for j in range(3)]
        return parts[1] + across(parts[0], -1) + across(parts[2], 1)

    charge = flat * image
    curvature = curve(charge)
    gain = 1.0 + bfe * curvature
    spread = charge * gain
    resid = weights * (couple(spread, kappa) - observed)
    spread_grad = couple(resid, [row[::-1] for row in kappa[::-1]])
    scaled = spread_grad * charge
    charge_grad = (spread_grad * gain + curve(scaled * bfe))[own]
    gout[:, 1] = (scaled * curvature)[own].reshape(nf, k, width)
    gout[:, 0] = (charge_grad * image[own]).reshape(nf, k, width)

    def scatter(i):
        other = lax.rem(f + i + 1, nf)
        return remote(gout.at[other], gin.at[f], rs_send.at[i], rs_recv.at[f], device(other, b))

    repeat(nf - 1, lambda i: scatter(i).start())
    gin[f] = gout[f]

    image_grad = charge_grad * flat[own]
    dint = dot3(image_grad * inv_total, gh[...], gl[...]) * (2.0 * norm)
    de = jnp.concatenate([e_real[own] * dint, e_imag[own] * dint], 0)
    nt = ((1,), (1,))
    z_real = dot3(de, bh[:, :width], bl[:, :width], nt)
    z_imag = dot3(de, bh[:, width:], bl[:, width:], nt)
    dm_real = z_real[:rd] + z_imag[rd:]
    dm_imag = z_real[rd:] - z_imag[:rd]
    right = jnp.concatenate(
        [jnp.concatenate([dm_real, dm_imag], 1), jnp.concatenate([dm_imag, -dm_real], 1)], 0
    )
    right_high, right_low = split(right)
    left_own = jnp.concatenate([a_real[own], a_imag[own]], 0).T
    left_high, left_low = split(left_own)
    dp = (
        mm(left_high, right_high) + mm(left_low, right_high) + mm(left_high, right_low)
    )
    dphase = pup[:, :NP] * dp[:, NP:] - pup[:, NP:] * dp[:, :NP]
    full_u = (2.0 * iota((NP, NP), 0) + 1.0) / NP - 1.0
    term = dphase
    by_power = []
    for power in range(DEGREE + 1):
        by_power.append(jnp.sum(term, 0, keepdims=True))
        if power < DEGREE:
            term = term * full_u
    by_power.append(jnp.zeros((2, NP), F32))
    by_row = jnp.concatenate(by_power, 0)
    sub = lax.broadcasted_iota(jnp.int32, (8, 128), 0)
    lane = lax.broadcasted_iota(jnp.int32, (8, 128), 1)
    modes = jnp.zeros((8, 128), F32)
    for q in range(DEGREE + 1):
        value = jnp.sum(by_row * lane_pow[q], 1, keepdims=True)
        for power in range(DEGREE + 1 - q):
            d = power + q
            here = (sub == power) & (lane == d * (d + 1) // 2 + power)
            modes = jnp.where(here, value, modes)
    modes = jnp.sum(modes, 0, keepdims=True)

    def fold(value):
        folded = jnp.sum(value.reshape(rd // 8, 8, width), 0)
        return sum(folded[:, j * 128 : (j + 1) * 128] for j in range(width // 128))

    def everything(folded):
        return jnp.sum(jnp.sum(folded, 0, keepdims=True), 1, keepdims=True)

    tile = jnp.where(sub == 3, modes, 0.0)
    resid_own = resid[own]
    shifted_resid = [across(resid_own, 1), resid_own, across(resid_own, -1)]
    for i in range(3):
        spread_rows = spread[HALO + i - 1 : HALO + rd + i - 1]
        for j in range(3):
            value = everything(fold(shifted_resid[j] * spread_rows))
            tile = jnp.where((sub == i) & (lane == j), value, tile)
    tile = jnp.where((sub == 4) & (lane == 0), everything(fold(image_grad * blurred_dot)), tile)
    outbox[...] = tile

    each_peer(lambda where: remote(outbox, inbox.at[me], box_send, box_recv, where).start())
    inbox[me] = tile

    def gathered(i):
        other = lax.rem(f + i + 1, nf)
        remote(gout.at[0], gin.at[other], rs_send.at[i], rs_recv.at[other], device(other, b)).wait_recv()

    repeat(nf - 1, gathered)
    summed = jnp.sum(gin[...], 0)
    gsum[...] = summed

    every = inbox.at[pl.ds(0, group - 1)]
    all_tiles = remote(every, every, box_send, box_recv, device(f, b))
    all_tiles.wait_recv()
    of_frame = jnp.sum(inbox[pl.ds(f * nb, nb)], 0)
    small[...] = jnp.where(sub == 4, of_frame, jnp.sum(inbox[...], 0))

    repeat(nf - 1, lambda i: map_same(i).wait_send())

    @pl.when(has_up)
    def _():
        repeat(h, lambda i: map_up(i).wait_send())
        ow_up().wait_send()

    @pl.when(has_down)
    def _():
        repeat(h, lambda i: map_down(i).wait_send())
        ow_down().wait_send()

    repeat(nf - 1, lambda i: scatter(i).wait_send())
    all_tiles.wait_send()


def finish(gsum, small, gflat, gbfe, gipc, gzern, gjit):
    gflat[0] = gsum[0]
    gbfe[0] = gsum[1]
    gipc[...] = small[0:3, 0:3]
    gzern[...] = small[3, : gzern.shape[0]]
    gjit[...] = small[4, 0:1]


def local(
    nf, nmap, npsf,
    observed, pixel_mask, ramp_counts, flat_map, bfe_map, ipc_kernel, zernike, jitter, sky_level, dither,
):
    _, rd, width = observed.shape
    k = flat_map.shape[1]
    group = nf * nmap * npsf
    h = HALO // k
    hbm = pl.BlockSpec(memory_space=pltpu.HBM)
    vmem = pl.BlockSpec(memory_space=pltpu.VMEM)
    dma = pltpu.SemaphoreType.DMA
    gsum, small = pl.pallas_call(
        functools.partial(kernel, nf, nmap, npsf, rd, k, width),
        out_shape=(
            jax.ShapeDtypeStruct((2, k, width), F32),
            jax.ShapeDtypeStruct((8, 128), F32),
        ),
        in_specs=[hbm] * 9,
        out_specs=(vmem, vmem),
        scratch_shapes=[
            pltpu.SMEM(zernike.shape, F32),
            pltpu.SMEM((2,), F32),
            pltpu.SMEM((1, 2), jnp.int32),
            pltpu.SMEM((3, 3), F32),
            pltpu.VMEM((nf + 2 * h, 2, k, width), F32),
            pltpu.VMEM((rd // 8 + 2, 2, 8, width), F32),
            pltpu.VMEM((rd, width), F32),
            pltpu.VMEM((rd, width), jnp.int32),
            pltpu.VMEM((rd, width), jnp.int32),
            pltpu.VMEM((NP, 2 * NP), F32),
            pltpu.VMEM((NP, 2 * NP), BF16),
            pltpu.VMEM((NP, 2 * NP), BF16),
            pltpu.VMEM((NP, 2 * width), BF16),
            pltpu.VMEM((NP, 2 * width), BF16),
            pltpu.VMEM((width, width), BF16),
            pltpu.VMEM((width, width), BF16),
            pltpu.VMEM((width, width), BF16),
            pltpu.VMEM((width, width), BF16),
            pltpu.VMEM((nf, 2, k, width), F32),
            pltpu.VMEM((nf, 2, k, width), F32),
            pltpu.VMEM((8, 128), F32),
            pltpu.VMEM((group, 8, 128), F32),
            dma((9,)),
            dma((nf,)),
            dma((2, h)),
            dma((nf + 2 * h,)),
            dma((2,)),
            dma((2,)),
            dma((nf,)),
            dma((nf,)),
            dma,
            dma,
        ],
        compiler_params=pltpu.CompilerParams(
            collective_id=0, has_side_effects=True, vmem_limit_bytes=VMEM_LIMIT
        ),
    )(zernike, jnp.concatenate([jitter, sky_level]), dither, ipc_kernel, flat_map, bfe_map, observed, pixel_mask, ramp_counts)
    return pl.pallas_call(
        finish,
        out_shape=(
            jax.ShapeDtypeStruct(flat_map.shape, F32),
            jax.ShapeDtypeStruct(bfe_map.shape, F32),
            jax.ShapeDtypeStruct(ipc_kernel.shape, F32),
            jax.ShapeDtypeStruct(zernike.shape, F32),
            jax.ShapeDtypeStruct(jitter.shape, F32),
        ),
        in_specs=[vmem] * 2,
        out_specs=(vmem,) * 5,
    )(gsum, small)


def solution(mesh):
    in_specs = (
        P(("groups", "frame"), ("map", "psf"), None),
        P(("groups", "frame"), ("map", "psf"), None),
        P(("groups", "frame"), ("map", "psf"), None),
        P(("groups", "map", "psf"), "frame", None),
        P(("groups", "map", "psf"), "frame", None),
        P("groups", None),
        P("groups"),
        P(("groups", "frame")),
        P(("groups", "frame")),
        P(("groups", "frame"), None),
    )
    out_specs = (
        P(("groups", "map", "psf"), "frame", None),
        P(("groups", "map", "psf"), "frame", None),
        P("groups", None),
        P("groups"),
        P(("groups", "frame")),
    )
    body = functools.partial(local, mesh.shape["frame"], mesh.shape["map"], mesh.shape["psf"])
    return jax.shard_map(body, mesh=mesh, in_specs=in_specs, out_specs=out_specs, check_vma=False)
```

```python
import functools
import math

import jax
import jax.numpy as jnp
import numpy as np
from jax import lax
from jax.experimental import pallas as pl
from jax.experimental.pallas import tpu as pltpu
from jax.sharding import PartitionSpec as P

NP = 256
NR = 16
HALO = 8
VMEM_LIMIT = 63 * 1024 * 1024
OVERSAMPLE = 32
AMPLITUDE = 2.0
IPC_CENTER = 0.8
DEGREE = 5
F32 = jnp.float32
BF16 = jnp.bfloat16
MESH = pl.DeviceIdType.MESH


def turn_polynomials():
    nodes = 0.125 * (1.0 + np.cos((np.arange(64) + 0.5) * np.pi / 64))
    root = np.sqrt(nodes)
    cos_fit = np.polynomial.Chebyshev.fit(nodes, np.cos(2 * np.pi * root), 7, domain=[0, 0.25])
    sin_fit = np.polynomial.Chebyshev.fit(nodes, np.sin(2 * np.pi * root) / root, 7, domain=[0, 0.25])
    as_power = np.polynomial.Polynomial
    return (
        [float(v) for v in cos_fit.convert(kind=as_power).coef],
        [float(v) for v in sin_fit.convert(kind=as_power).coef],
    )


COS_COEF, SIN_COEF = turn_polynomials()


def horner(coefs, x):
    acc = jnp.full_like(x, coefs[-1])
    for value in coefs[-2::-1]:
        acc = acc * x + value
    return acc


def cos_sin_turns(turns):
    rest = turns - jnp.floor(turns + 0.5)
    square = rest * rest
    return horner(COS_COEF, square), rest * horner(SIN_COEF, square)


def bfe_weights():
    table = np.zeros((3, 3))
    total = 0.0
    for i in range(-2, 3):
        for j in range(-2, 3):
            if i or j:
                table[abs(i), abs(j)] = 1.0 / (i * i + j * j)
                total += 1.0 / (i * i + j * j)
    table[0, 0] = -total
    return (table / total).tolist()


BFE = bfe_weights()


def split(x):
    high = x.astype(BF16)
    return high, (x - high.astype(F32)).astype(BF16)


def mm(a, b, dims=((1,), (0,))):
    return lax.dot_general(a, b, (dims, ((), ())), preferred_element_type=F32)


def dot3(a, b_high, b_low, dims=((1,), (0,))):
    high, low = split(a)
    n = a.shape[0]
    both = mm(jnp.concatenate([high, low], 0), b_high, dims)
    return both[:n] + both[n:] + mm(high, b_low, dims)


def iota(shape, axis):
    return lax.broadcasted_iota(jnp.int32, shape, axis).astype(F32)


def repeat(count, body):
    if count <= 16:
        for i in range(count):
            body(i)
    else:
        lax.fori_loop(0, count, lambda i, c: (body(i), c)[1], 0)


def kernel(
    nf, nmap, npsf, rd, k, width,
    zern_in, jit_in, sky_in, dith_in, ipc_in, flat_in, bfe_in, obs_in, mask_in, count_in,
    gsum, small,
    zern, jit, sky, dith, ipc,
    maps, ow, obs_v, mask_v, count_v, pup, ph, plo, bh, bl, gh, gl, dh, dl, gout, gin, outbox, inbox,
    local_sem, map_send, pass_send, map_recv, ow_send, ow_recv, rs_send, rs_recv, box_send, box_recv,
):
    nb = nmap * npsf
    group = nf * nb
    rows = rd + 2 * HALO
    h = HALO // k
    f = lax.axis_index("frame")
    m = lax.axis_index("map")
    p = lax.axis_index("psf")
    b = m * npsf + p
    me = f * nb + b

    def device(frame, block):
        return {"frame": frame, "map": lax.div(block, npsf), "psf": lax.rem(block, npsf)}

    def wrap(value, count):
        return jnp.where(value >= count, value - count, value)

    others = [(i, j) for i in range(nmap) for j in range(npsf)]

    def each_peer(body):
        def of_frame(step, spots):
            for i, j in spots:
                body({"frame": wrap(f + step, nf), "map": wrap(m + i, nmap), "psf": wrap(p + j, npsf)})

        repeat(nf - 1, lambda step: of_frame(step + 1, others))
        of_frame(0, others[1:])

    barrier = pltpu.get_barrier_semaphore()
    each_peer(lambda where: pl.semaphore_signal(barrier, inc=1, device_id=where, device_id_type=MESH))

    loads = [
        pltpu.make_async_copy(flat_in.at[0], maps.at[h + f, 0], local_sem.at[0]),
        pltpu.make_async_copy(bfe_in.at[0], maps.at[h + f, 1], local_sem.at[1]),
        pltpu.make_async_copy(obs_in.at[0], obs_v, local_sem.at[2]),
        pltpu.make_async_copy(mask_in.at[0], mask_v, local_sem.at[3]),
        pltpu.make_async_copy(count_in.at[0], count_v, local_sem.at[4]),
        pltpu.make_async_copy(zern_in, zern, local_sem.at[5]),
        pltpu.make_async_copy(jit_in, jit, local_sem.at[6]),
        pltpu.make_async_copy(sky_in, sky, local_sem.at[7]),
        pltpu.make_async_copy(dith_in, dith, local_sem.at[8]),
        pltpu.make_async_copy(ipc_in, ipc, local_sem.at[9]),
    ]
    for load in loads:
        load.start()

    def remote(src, dst, send, recv, where):
        return pltpu.make_async_remote_copy(
            src_ref=src, dst_ref=dst, send_sem=send, recv_sem=recv, device_id=where, device_id_type=MESH
        )

    has_up = b > 0
    has_down = b < nb - 1
    blocks = rd // 8
    mine = maps.at[h + f]

    def ow_up():
        return remote(ow.at[1], ow.at[1 + blocks], ow_send.at[0], ow_recv.at[1], device(f, b - 1))

    def ow_down():
        return remote(ow.at[blocks], ow.at[0], ow_send.at[1], ow_recv.at[0], device(f, b + 1))

    def map_same(i):
        return remote(mine, maps.at[h + f], map_send.at[i], map_recv.at[h + f], device(lax.rem(f + i + 1, nf), b))

    def map_down(i):
        return remote(maps.at[nf + i], maps.at[i], pass_send.at[1, i], map_recv.at[i], device(f, b + 1))

    def map_up(i):
        slot = h + nf + i
        return remote(maps.at[h + i], maps.at[slot], pass_send.at[0, i], map_recv.at[slot], device(f, b - 1))

    def arrive(i):
        @pl.when(i != f)
        def _():
            remote(mine, maps.at[h + i], map_send.at[0], map_recv.at[h + i], device(f, b)).wait_recv()

    @pl.when(b == 0)
    def _():
        maps[0:h] = jnp.zeros((h, 2, k, width), F32)
        ow[0:1] = jnp.zeros((1, 2, 8, width), F32)

    @pl.when(b == nb - 1)
    def _():
        maps[h + nf : 2 * h + nf] = jnp.zeros((h, 2, k, width), F32)
        ow[1 + blocks : 2 + blocks] = jnp.zeros((1, 2, 8, width), F32)

    for load in loads[:2]:
        load.wait()
    pl.semaphore_wait(barrier, group - 1)
    repeat(nf - 1, lambda i: map_same(i).start())

    for load in loads[2:]:
        load.wait()
    scale = 1.0 / (NR * math.sqrt(nf))
    ow[1 : 1 + blocks, 0] = obs_v[...].reshape(blocks, 8, width)
    weight = mask_v[...].astype(F32) * count_v[...].astype(F32) * scale
    ow[1 : 1 + blocks, 1] = weight.reshape(blocks, 8, width)

    @pl.when(has_up)
    def _():
        ow_up().start()

    @pl.when(has_down)
    def _():
        ow_down().start()

    step = 64
    lane_u = (2.0 * iota((1, NP), 1) + 1.0) / NP - 1.0
    lane_pow = [jnp.ones((1, NP), F32)]
    for _ in range(DEGREE):
        lane_pow.append(lane_pow[-1] * lane_u)
    per_power = []
    for power in range(DEGREE + 1):
        acc = jnp.zeros((1, NP), F32)
        for q in range(DEGREE + 1 - power):
            d = power + q
            acc = acc + (zern[d * (d + 1) // 2 + power] * (0.5 / math.pi)) * lane_pow[q]
        per_power.append(acc)

    def pupil(i, carry):
        start = pl.multiple_of(i * step, step)
        u = (2.0 * (iota((step, NP), 0) + (i * step).astype(F32)) + 1.0) / NP - 1.0
        turns = jnp.broadcast_to(per_power[DEGREE], (step, NP))
        for power in range(DEGREE - 1, -1, -1):
            turns = turns * u + per_power[power]
        radius = u * u + lane_u * lane_u
        inside = jnp.where((radius <= 1.0) & (radius >= 0.09), 1.0, 0.0)
        real, imag = cos_sin_turns(turns)
        for half, value in enumerate((real * inside, imag * inside)):
            at = (pl.ds(start, step), pl.ds(half * NP, NP))
            high, low = split(value)
            pup[at] = value
            ph[at] = high
            plo[at] = low
        return carry

    lax.fori_loop(0, NP // step, pupil, 0)

    rho = nb * rd / 2.0 + dith[0, 0].astype(F32)
    chi = width / 2.0 + dith[0, 1].astype(F32)
    unit = 1.0 / (2 * OVERSAMPLE * NP)
    col_step = 32

    def column(i, carry):
        start = pl.multiple_of(i * col_step, col_step)
        index = 2.0 * (iota((col_step, width), 0) + (i * col_step).astype(F32)) + (1.0 - NP)
        turns = index * (chi - iota((col_step, width), 1)) * unit
        for half, value in enumerate(cos_sin_turns(turns)):
            at = (pl.ds(start, col_step), pl.ds(half * width, width))
            high, low = split(value)
            bh[at] = high
            bl[at] = low
        return carry

    lax.fori_loop(0, NP // col_step, column, 0)

    sigma = jnp.full((1, width), jit[0], F32)
    inv = 1.0 / sigma
    inv2 = inv * inv
    cube = inv2 * inv

    def blur(i, carry):
        total, total_dot = carry
        start = pl.multiple_of(i * col_step, col_step)
        off = iota((col_step, width), 0) + (i * col_step).astype(F32) - iota((col_step, width), 1)
        square = off * off
        value = jnp.exp(square * (-0.5 * inv2))
        slope = value * (square * cube)
        at = (pl.ds(start, col_step), slice(None))
        gh[at], gl[at] = split(value)
        dh[at], dl[at] = split(slope)
        total = total + jnp.sum(value.reshape(col_step // 8, 8, width), 0)
        total_dot = total_dot + jnp.sum(slope.reshape(col_step // 8, 8, width), 0)
        return total, total_dot

    zero8 = jnp.zeros((8, width), F32)
    total, total_dot = lax.fori_loop(0, width // col_step, blur, (zero8, zero8))
    inv_total = 1.0 / jnp.sum(total, 0, keepdims=True)
    ratio = jnp.sum(total_dot, 0, keepdims=True) * inv_total

    first = (b * rd).astype(F32) - float(HALO)
    row_angle = (2.0 * iota((rows, NP), 1) + (1.0 - NP)) * (rho - first - iota((rows, NP), 0)) * unit
    a_real, a_imag = cos_sin_turns(row_angle)
    left = jnp.concatenate([a_real, a_imag], 0)
    x = dot3(left, ph[...], plo[...])
    mid = jnp.concatenate(
        [x[:rows, :NP] - x[rows:, NP:], x[:rows, NP:] + x[rows:, :NP]], 0
    )
    y = dot3(mid, bh[...], bl[...])
    e_real = y[:rows, :width] - y[rows:, width:]
    e_imag = y[:rows, width:] + y[rows:, :width]
    norm = (AMPLITUDE / NP**2) ** 2
    intensity = (e_real * e_real + e_imag * e_imag) * norm
    own = slice(HALO, HALO + rd)

    repeat(h, arrive)
    repeat(h, lambda i: arrive(nf - h + i))

    @pl.when(has_up)
    def _():
        repeat(h, lambda i: map_up(i).start())

    @pl.when(has_down)
    def _():
        repeat(h, lambda i: map_down(i).start())

    blurred = dot3(intensity, gh[...], gl[...]) * inv_total
    blurred_dot = dot3(intensity[own], dh[...], dl[...]) * inv_total - blurred[own] * ratio
    image = blurred + sky[0]

    repeat(nf - 2 * h, lambda i: arrive(h + i))

    @pl.when(has_up)
    def _():
        repeat(h, lambda i: remote(mine, maps.at[i], map_send.at[0], map_recv.at[i], device(f, b)).wait_recv())
        ow_down().wait_recv()

    @pl.when(has_down)
    def _():
        repeat(
            h,
            lambda i: remote(
                mine, maps.at[h + nf + i], map_send.at[0], map_recv.at[h + nf + i], device(f, b)
            ).wait_recv(),
        )
        ow_up().wait_recv()

    flat = maps[:, 0].reshape(rows, width)
    bfe = maps[:, 1].reshape(rows, width)
    observed = ow[:, 0].reshape(rows, width)
    weights = ow[:, 1].reshape(rows, width)
    col = lax.broadcasted_iota(jnp.int32, (rows, width), 1)

    def down(value, d):
        return pltpu.roll(value, (-d) % value.shape[0], 0)

    def across(value, d):
        rolled = pltpu.roll(value, (-d) % width, 1)
        at = col[: value.shape[0]]
        return jnp.where(at < width - d if d > 0 else at >= -d, rolled, 0.0)

    def curve(value):
        one = down(value, 1) + down(value, -1)
        two = down(value, 2) + down(value, -2)
        parts = [BFE[0][j] * value + BFE[1][j] * one + BFE[2][j] * two for j in range(3)]
        return (
            parts[0]
            + (across(parts[1], 1) + across(parts[1], -1))
            + (across(parts[2], 2) + across(parts[2], -2))
        )

    kappa = [[ipc[i, j] + (IPC_CENTER if i == j == 1 else 0.0) for j in range(3)] for i in range(3)]

    def couple(value, table):
        shifted = [down(value, -1), value, down(value, 1)]
        parts = [sum(table[i][j] * shifted[i] for i in range(3)) for j in range(3)]
        return parts[1] + across(parts[0], -1) + across(parts[2], 1)

    charge = flat * image
    curvature = curve(charge)
    gain = 1.0 + bfe * curvature
    spread = charge * gain
    resid = weights * (couple(spread, kappa) - observed)
    spread_grad = couple(resid, [row[::-1] for row in kappa[::-1]])
    scaled = spread_grad * charge
    charge_grad = (spread_grad * gain + curve(scaled * bfe))[own]
    gout[:, 1] = (scaled * curvature)[own].reshape(nf, k, width)
    gout[:, 0] = (charge_grad * image[own]).reshape(nf, k, width)

    def scatter(i):
        other = lax.rem(f + i + 1, nf)
        return remote(gout.at[other], gin.at[f], rs_send.at[i], rs_recv.at[f], device(other, b))

    repeat(nf - 1, lambda i: scatter(i).start())
    gin[f] = gout[f]

    image_grad = charge_grad * flat[own]
    dint = dot3(image_grad * inv_total, gh[...], gl[...]) * (2.0 * norm)
    de = jnp.concatenate([e_real[own] * dint, e_imag[own] * dint], 0)
    nt = ((1,), (1,))
    z_real = dot3(de, bh[:, :width], bl[:, :width], nt)
    z_imag = dot3(de, bh[:, width:], bl[:, width:], nt)
    dm_real = z_real[:rd] + z_imag[rd:]
    dm_imag = z_real[rd:] - z_imag[:rd]
    right = jnp.concatenate(
        [jnp.concatenate([dm_real, dm_imag], 1), jnp.concatenate([dm_imag, -dm_real], 1)], 0
    )
    right_high, right_low = split(right)
    left_own = jnp.concatenate([a_real[own], a_imag[own]], 0).T
    left_high, left_low = split(left_own)
    dp = (
        mm(left_high, right_high) + mm(left_low, right_high) + mm(left_high, right_low)
    )
    dphase = pup[:, :NP] * dp[:, NP:] - pup[:, NP:] * dp[:, :NP]
    full_u = (2.0 * iota((NP, NP), 0) + 1.0) / NP - 1.0
    term = dphase
    by_power = []
    for power in range(DEGREE + 1):
        by_power.append(jnp.sum(term, 0, keepdims=True))
        if power < DEGREE:
            term = term * full_u
    by_power.append(jnp.zeros((2, NP), F32))
    by_row = jnp.concatenate(by_power, 0)
    sub = lax.broadcasted_iota(jnp.int32, (8, 128), 0)
    lane = lax.broadcasted_iota(jnp.int32, (8, 128), 1)
    modes = jnp.zeros((8, 128), F32)
    for q in range(DEGREE + 1):
        value = jnp.sum(by_row * lane_pow[q], 1, keepdims=True)
        for power in range(DEGREE + 1 - q):
            d = power + q
            here = (sub == power) & (lane == d * (d + 1) // 2 + power)
            modes = jnp.where(here, value, modes)
    modes = jnp.sum(modes, 0, keepdims=True)

    def fold(value):
        folded = jnp.sum(value.reshape(rd // 8, 8, width), 0)
        return sum(folded[:, j * 128 : (j + 1) * 128] for j in range(width // 128))

    def everything(folded):
        return jnp.sum(jnp.sum(folded, 0, keepdims=True), 1, keepdims=True)

    tile = jnp.where(sub == 3, modes, 0.0)
    resid_own = resid[own]
    shifted_resid = [across(resid_own, 1), resid_own, across(resid_own, -1)]
    for i in range(3):
        spread_rows = spread[HALO + i - 1 : HALO + rd + i - 1]
        for j in range(3):
            value = everything(fold(shifted_resid[j] * spread_rows))
            tile = jnp.where((sub == i) & (lane == j), value, tile)
    tile = jnp.where((sub == 4) & (lane == 0), everything(fold(image_grad * blurred_dot)), tile)
    outbox[...] = tile

    each_peer(lambda where: remote(outbox, inbox.at[me], box_send, box_recv, where).start())
    inbox[me] = tile

    def gathered(i):
        other = lax.rem(f + i + 1, nf)
        remote(gout.at[0], gin.at[other], rs_send.at[i], rs_recv.at[other], device(other, b)).wait_recv()

    repeat(nf - 1, gathered)
    summed = jnp.sum(gin[...], 0)
    gsum[...] = summed

    every = inbox.at[pl.ds(0, group - 1)]
    all_tiles = remote(every, every, box_send, box_recv, device(f, b))
    all_tiles.wait_recv()
    of_frame = jnp.sum(inbox[pl.ds(f * nb, nb)], 0)
    small[...] = jnp.where(sub == 4, of_frame, jnp.sum(inbox[...], 0))

    repeat(nf - 1, lambda i: map_same(i).wait_send())

    @pl.when(has_up)
    def _():
        repeat(h, lambda i: map_up(i).wait_send())
        ow_up().wait_send()

    @pl.when(has_down)
    def _():
        repeat(h, lambda i: map_down(i).wait_send())
        ow_down().wait_send()

    repeat(nf - 1, lambda i: scatter(i).wait_send())
    all_tiles.wait_send()


def finish(gsum, small, gflat, gbfe, gipc, gzern, gjit):
    gflat[0] = gsum[0]
    gbfe[0] = gsum[1]
    gipc[...] = small[0:3, 0:3]
    gzern[...] = small[3, : gzern.shape[0]]
    gjit[...] = small[4, 0:1]


def local(
    nf, nmap, npsf,
    observed, pixel_mask, ramp_counts, flat_map, bfe_map, ipc_kernel, zernike, jitter, sky_level, dither,
):
    _, rd, width = observed.shape
    k = flat_map.shape[1]
    group = nf * nmap * npsf
    h = HALO // k
    hbm = pl.BlockSpec(memory_space=pltpu.HBM)
    vmem = pl.BlockSpec(memory_space=pltpu.VMEM)
    dma = pltpu.SemaphoreType.DMA
    gsum, small = pl.pallas_call(
        functools.partial(kernel, nf, nmap, npsf, rd, k, width),
        out_shape=(
            jax.ShapeDtypeStruct((2, k, width), F32),
            jax.ShapeDtypeStruct((8, 128), F32),
        ),
        in_specs=[hbm] * 10,
        out_specs=(vmem, vmem),
        scratch_shapes=[
            pltpu.SMEM(zernike.shape, F32),
            pltpu.SMEM((1,), F32),
            pltpu.SMEM((1,), F32),
            pltpu.SMEM((1, 2), jnp.int32),
            pltpu.SMEM((3, 3), F32),
            pltpu.VMEM((nf + 2 * h, 2, k, width), F32),
            pltpu.VMEM((rd // 8 + 2, 2, 8, width), F32),
            pltpu.VMEM((rd, width), F32),
            pltpu.VMEM((rd, width), jnp.int32),
            pltpu.VMEM((rd, width), jnp.int32),
            pltpu.VMEM((NP, 2 * NP), F32),
            pltpu.VMEM((NP, 2 * NP), BF16),
            pltpu.VMEM((NP, 2 * NP), BF16),
            pltpu.VMEM((NP, 2 * width), BF16),
            pltpu.VMEM((NP, 2 * width), BF16),
            pltpu.VMEM((width, width), BF16),
            pltpu.VMEM((width, width), BF16),
            pltpu.VMEM((width, width), BF16),
            pltpu.VMEM((width, width), BF16),
            pltpu.VMEM((nf, 2, k, width), F32),
            pltpu.VMEM((nf, 2, k, width), F32),
            pltpu.VMEM((8, 128), F32),
            pltpu.VMEM((group, 8, 128), F32),
            dma((10,)),
            dma((nf,)),
            dma((2, h)),
            dma((nf + 2 * h,)),
            dma((2,)),
            dma((2,)),
            dma((nf,)),
            dma((nf,)),
            dma,
            dma,
        ],
        compiler_params=pltpu.CompilerParams(
            collective_id=0, has_side_effects=True, vmem_limit_bytes=VMEM_LIMIT
        ),
    )(zernike, jitter, sky_level, dither, ipc_kernel, flat_map, bfe_map, observed, pixel_mask, ramp_counts)
    return pl.pallas_call(
        finish,
        out_shape=(
            jax.ShapeDtypeStruct(flat_map.shape, F32),
            jax.ShapeDtypeStruct(bfe_map.shape, F32),
            jax.ShapeDtypeStruct(ipc_kernel.shape, F32),
            jax.ShapeDtypeStruct(zernike.shape, F32),
            jax.ShapeDtypeStruct(jitter.shape, F32),
        ),
        in_specs=[vmem] * 2,
        out_specs=(vmem,) * 5,
    )(gsum, small)


def solution(mesh):
    in_specs = (
        P(("groups", "frame"), ("map", "psf"), None),
        P(("groups", "frame"), ("map", "psf"), None),
        P(("groups", "frame"), ("map", "psf"), None),
        P(("groups", "map", "psf"), "frame", None),
        P(("groups", "map", "psf"), "frame", None),
        P("groups", None),
        P("groups"),
        P(("groups", "frame")),
        P(("groups", "frame")),
        P(("groups", "frame"), None),
    )
    out_specs = (
        P(("groups", "map", "psf"), "frame", None),
        P(("groups", "map", "psf"), "frame", None),
        P("groups", None),
        P("groups"),
        P(("groups", "frame")),
    )
    body = functools.partial(local, mesh.shape["frame"], mesh.shape["map"], mesh.shape["psf"])
    return jax.shard_map(body, mesh=mesh, in_specs=in_specs, out_specs=out_specs, check_vma=False)
```
